128 devices in a mesh: gx: 8 (over z, x_hi), gy: 16 (over x_lo, y, core).
Axes of the slice: x: 4 (x_hi: 2, x_lo: 2; x = x_hi * 2 + x_lo), y: 4, z: 4, core: 2. Of those that a mesh axis runs over, the one named last changes fastest.
Arguments:
- velocity: bfloat16 [3, 64, 1024, 576], P(None, 'gx', 'gy'), may hold values from -6 to 6
- viscosity: bfloat16 [64, 1024, 576], P('gx', 'gy'), may hold values from 0.019897461 to 0.19921875
- tap_cell: int32 [128, 320], P(('gx', 'gy')), may hold values from 0 to 294911
- tap_block: int32 [128, 320], P(('gx', 'gy')), may hold values from 0 to 511
- block_slot: int32 [512], replicated, may hold values from 0 to 511, each once
Outputs:
- new_velocity: bfloat16 [3, 64, 1024, 576], P(None, 'gx', 'gy')
- epoch_max: float32 [512], P(('gx', 'gy'))
The draws below stay inside these ranges and needn't reach their ends.
Inputs may be any that keep to these rules, and one draw needn't show every extreme that they name: `tap_cell`: each index lies in the brick of 8 x 64 x 576 cells of the device that holds the row, flattened with x slowest and z fastest.
All inputs are finite; a program needn't handle non-finite values.
Results may differ from the reference program's by a relative error of at most 0.0078.
Values may be sent and summed in bfloat16 or wider, within the bound.
No kernel may reach another device: no remote copies, remote signals or barrier semaphores. Data moves between devices by JAX's collectives and lax.ppermute only.
A program may use at most 64 MiB of HBM per device.

```python
import math
import jax
import jax.numpy as jnp
import numpy as np
from jax import lax

CX = 8
CY = 64
NZ = 576
TAPS_DEV = 320
NX = 64
NY = 1024
BLOCKS = 512
N_GX = 8
N_GY = 16


def with_ends(array, key, smallest, top_value):
    extent = array.shape
    place = [jax.random.randint(jax.random.fold_in(key, axis), (), 0, extent[axis]) for axis in range(len(extent))]
    array = array.at[tuple(place)].set(smallest)
    longest = extent.index(max(extent))
    place[longest] = (place[longest] + 1) % extent[longest]
    return array.at[tuple(place)].set(top_value)


def levels(own_key, shape, shards, low, top_value):
    loudness = 1.0
    for dim, parts in shards:
        draws = jax.random.uniform(jax.random.fold_in(jax.random.fold_in(own_key, 6), dim), (parts,), jnp.float32, low / len(shards), top_value / len(shards))
        loudness = loudness * jnp.repeat(jnp.exp(draws), shape[dim] // parts).reshape((-1,) + (1,) * (len(shape) - 1 - dim))
    return loudness


def cumulative_ranks(number_of, skew):
    portions = [(1 << 20) // math.isqrt(grade ** skew) + 1 for grade in range(1, number_of + 1)]
    deviation = 1 + sum(portions) // (1 << 30)
    return np.cumsum(np.array([max(1, weight // deviation) for weight in portions]))


def ranked(key, dims, number_of, slope):
    listing = cumulative_ranks(number_of, slope)
    ticket = jax.random.randint(jax.random.fold_in(key, 1), dims, 0, int(listing[number_of - 1]))
    grade = jnp.searchsorted(jnp.asarray(listing, jnp.int32), ticket, side="right")
    return jax.random.permutation(jax.random.fold_in(key, 2), number_of)[grade].astype(jnp.int32)


def gaussian(key, extent, scale, reach, shards=(), kind=jnp.bfloat16):
    gain = levels(key, extent, shards, -0.22, 0.18) if shards else 1.0
    array = jax.random.normal(key, extent, jnp.float32) * scale * gain
    return jnp.minimum(jnp.maximum(array, -reach), reach).astype(kind)


def setup_inputs(seed: int = 0) -> dict:
    splits = jax.random.split(jax.random.key(seed), 6)
    return {
        "velocity": gaussian(splits[0], (3, NX, NY, NZ), 1.0, 6.0, ((1, 8), (2, 16))),
        "viscosity": jnp.clip(jnp.exp(math.log(0.19921875) - 2.3038113 * jax.random.uniform(splits[1], (NX, NY, NZ), jnp.float32) ** levels(splits[1], (NX, NY, NZ), ((0, 8), (1, 16)), -0.2, 0.2)), 0.019897461, 0.19921875).astype(jnp.bfloat16),
        "tap_cell": with_ends(jax.random.randint(splits[2], (N_GX * N_GY, TAPS_DEV), 0, CX * CY * NZ), jax.random.fold_in(splits[2], 1), 0, (CX * CY * NZ) - 1).astype(jnp.int32),
        "tap_block": with_ends(ranked(splits[3], (N_GX * N_GY, TAPS_DEV), BLOCKS, 2), jax.random.fold_in(splits[3], 3), 0, BLOCKS - 1).astype(jnp.int32),
        "block_slot": jax.random.permutation(splits[4], BLOCKS).astype(jnp.int32),
    }


step_size = 0.3


def shifted(field, step_x, step_y, step_z):
    return field[..., 1 + step_x:field.shape[-3] - 1 + step_x, 1 + step_y:field.shape[-2] - 1 + step_y, 1 + step_z:field.shape[-1] - 1 + step_z]


def advance(flow_pad, visc_pad):
    flow = flow_pad.astype(jnp.float32)
    viscous = visc_pad.astype(jnp.float32)
    flow = jnp.concatenate([jnp.zeros_like(flow[..., :1]), flow, flow[..., -1:]], axis=-1)
    viscous = jnp.concatenate([viscous[..., :1], viscous, viscous[..., -1:]], axis=-1)
    offsets = ((1, 0, 0), (0, 1, 0), (0, 0, 1))
    centre_visc = shifted(viscous, 0, 0, 0)
    centre = shifted(flow, 0, 0, 0)
    results = []
    for channel in range(3):
        centre_val = centre[channel]
        change = jnp.zeros_like(centre_val)
        for axis_id, (step_x, step_y, step_z) in enumerate(offsets):
            above_cell = shifted(flow[channel], step_x, step_y, step_z)
            below_cell = shifted(flow[channel], -step_x, -step_y, -step_z)
            visc_above = shifted(viscous, step_x, step_y, step_z)
            visc_below = shifted(viscous, -step_x, -step_y, -step_z)
            change = change + 0.5 * (centre_visc + visc_above) * (above_cell - centre_val)
            change = change - 0.5 * (centre_visc + visc_below) * (centre_val - below_cell)
            change = change - 0.5 * centre[axis_id] * (above_cell - below_cell)
        results.append((centre_val + step_size * change).astype(jnp.bfloat16))
    return jnp.stack(results, 0)


def tap_energy(state, tap_cell):
    energy = jnp.sum(jnp.square(state.astype(jnp.float32)), axis=0)
    device = jnp.arange(N_GX * N_GY, dtype=jnp.int32)[:, None]
    row_x = (device // N_GY) * CX + tap_cell // (CY * NZ)
    row_y = (device % N_GY) * CY + (tap_cell // NZ) % CY
    row_z = tap_cell % NZ
    return energy[row_x, row_y, row_z]


def reference(velocity, viscosity, tap_cell, tap_block, block_slot):
    viscous = jnp.concatenate([viscosity[-1:], viscosity, viscosity[:1]], axis=0)
    viscous = jnp.concatenate([viscous[:, -1:], viscous, viscous[:, :1]], axis=1)
    state = velocity
    peaks = jnp.zeros(tap_cell.shape, jnp.float32)
    for step in range(2):
        flow = jnp.concatenate([state[:, -1:], state, state[:, :1]], axis=1)
        flow = jnp.concatenate([flow[:, :, -1:], flow, flow[:, :, :1]], axis=2)

        def one_block(index):
            start = (index * CX).astype(jnp.int32)
            return advance(lax.dynamic_slice_in_dim(flow, start, CX + 2, 1), lax.dynamic_slice_in_dim(viscous, start, CX + 2, 0))

        blocks = lax.map(one_block, jnp.arange(N_GX, dtype=jnp.int32))
        state = jnp.transpose(blocks, (1, 0, 2, 3, 4)).reshape(3, NX, NY, NZ)
        peaks = jnp.maximum(peaks, tap_energy(state, tap_cell))
    block_peak = jnp.zeros((BLOCKS,), jnp.float32).at[tap_block.reshape(-1)].max(peaks.reshape(-1))
    epoch_max = jnp.zeros((BLOCKS,), jnp.float32).at[block_slot].set(block_peak)
    return state, epoch_max
```

```python
import jax
import jax.numpy as jnp
from jax import lax
from jax.experimental import pallas as pl
from jax.experimental.pallas import tpu as pltpu
from jax.sharding import PartitionSpec as P

F32 = jnp.float32
BF16 = jnp.bfloat16
HALF = 0.15
TOP = 8
CHUNK = 16
PADDED = 640


def put(pad, field, x, row, value, low):
    rows, nz = value.shape
    pad[field, x, row : row + rows, :nz] = value
    lane = lax.broadcasted_iota(jnp.int32, (rows, PADDED - nz), 1)
    above = jnp.broadcast_to(value[:, nz - 1 : nz], lane.shape)
    below = jnp.broadcast_to(value[:, :1], lane.shape) if low else jnp.zeros(lane.shape, F32)
    pad[field, x, row : row + rows, nz:] = jnp.where(lane == PADDED - nz - 1, below, above)


def put_layer(pad, x, read_velocity, read_viscosity, ny):
    for k in range(0, ny, CHUNK):
        for c in range(3):
            put(pad, c, x, TOP + k, read_velocity(c, k).astype(F32), False)
        if read_viscosity is not None:
            put(pad, 3, x, TOP + k, read_viscosity(k).astype(F32) * HALF, True)


def update(pad, x, row):
    here = [pad[f, x, row : row + CHUNK, :] for f in range(4)]
    total = [here[0], here[1], here[2]]
    for d in range(3):
        drift = here[d] * HALF
        if d == 2:
            above = [pltpu.roll(v, PADDED - 1, 1) for v in here]
            high = above[3] + here[3]
            low = pltpu.roll(high, 1, 1)
            ups = [above[c] - here[c] for c in range(3)]
            downs = [pltpu.roll(u, 1, 1) for u in ups]
        else:
            if d == 0:
                above = [pad[f, x + 1, row : row + CHUNK, :] for f in range(4)]
                below = [pad[f, x - 1, row : row + CHUNK, :] for f in range(4)]
            else:
                above = [pad[f, x, row + 1 : row + 1 + CHUNK, :] for f in range(4)]
                below = [pad[f, x, row - 1 : row - 1 + CHUNK, :] for f in range(4)]
            high = above[3] + here[3]
            low = below[3] + here[3]
            ups = [above[c] - here[c] for c in range(3)]
            downs = [here[c] - below[c] for c in range(3)]
        plus = high - drift
        minus = low + drift
        for c in range(3):
            total[c] = total[c] + (plus * ups[c] - minus * downs[c])
    return total


def first_step(vel, visc, ylo, yhi, s1, edge_lo, edge_hi, part, rows, pad):
    _, nx, ny, nz = vel.shape

    def fill(x, _):
        put_layer(pad, x + 1, lambda c, k: vel[c, x, k : k + CHUNK, :], lambda k: visc[x, k : k + CHUNK, :], ny)
        return 0

    lax.fori_loop(0, nx, fill, 0)
    for ghost, row in ((ylo, TOP - 1), (yhi, TOP + ny)):
        for f in range(4):
            value = ghost[f].astype(F32) * (HALF if f == 3 else 1.0)
            for x in range(nx):
                put(pad, f, x + 1, row, value[x : x + 1], f == 3)
    pad[:, 0] = pad[:, 1]
    pad[:, nx + 1] = pad[:, nx]

    def layer(x, side):
        for k in range(0, ny, CHUNK):
            new = update(pad, x + 1, TOP + k)
            for c in range(3):
                value = new[c][:, :nz]
                s1[c, x, k : k + CHUNK, :] = value.astype(BF16)
                if side is not None:
                    (edge_lo, edge_hi)[side][c, k : k + CHUNK, :] = value.astype(BF16)
                    part[side, c, k : k + CHUNK, :] = value
                if k == 0:
                    rows[0, c, pl.ds(x, 1), :] = value[:1]
                if k == ny - CHUNK:
                    rows[1, c, pl.ds(x, 1), :] = value[CHUNK - 1 :]

    layer(0, 0)
    layer(nx - 1, 1)

    def middle(x, _):
        layer(x, None)
        return 0

    lax.fori_loop(1, nx - 1, middle, 0)


def first_edges(part, own_lo, own_hi, alo, ahi, rows, edges, extra, face_lo, face_hi):
    _, _, ny, nz = part.shape
    nx = rows.shape[2]
    faces = [[rows[i, c] for c in range(3)] for i in range(2)]
    line = lax.broadcasted_iota(jnp.int32, (nx, nz), 0)
    for side, (own, ghost) in enumerate(((own_lo, alo), (own_hi, ahi))):
        sign = 1.0 if side else -1.0
        for k in range(0, ny, CHUNK):
            mine = [own[f, k : k + CHUNK, :].astype(F32) for f in range(4)]
            far = [ghost[f, k : k + CHUNK, :].astype(F32) for f in range(4)]
            both = (mine[3] + far[3]) * HALF
            near_coef = both - sign * HALF * mine[0]
            far_coef = both + sign * HALF * far[0]
            for c in range(3):
                gap = far[c] - mine[c]
                value = part[side, c, k : k + CHUNK, :] + near_coef * gap
                edges[side, c, k : k + CHUNK, :] = value.astype(BF16)
                extra[side, c, k : k + CHUNK, :] = -far_coef * gap
                x = (nx - 1) * side
                if k == 0:
                    faces[0][c] = jnp.where(line == x, jnp.broadcast_to(value[:1], line.shape), faces[0][c])
                if k == ny - CHUNK:
                    faces[1][c] = jnp.where(line == x, jnp.broadcast_to(value[CHUNK - 1 :], line.shape), faces[1][c])
    for c in range(3):
        face_lo[c] = faces[0][c].astype(BF16)
        face_hi[c] = faces[1][c].astype(BF16)


def energies(hot, states, z, nz):
    total = None
    for state in states:
        value = jnp.dot(hot, state, preferred_element_type=F32)
        total = value * value if total is None else total + value * value
    lane = lax.broadcasted_iota(jnp.int32, total.shape, 1)
    return jnp.max(jnp.where(lane == z, total, 0.0), axis=1, keepdims=True)


def second_step(s1, edges, visc, alo, ahi, ylo, yhi, row_of, z_of, late_of, block_of, slots,
                s2, quasi, quasi_rows, blocks, coef_x, coef_y, hot_late, slot_of, peaks, pad, state):
    _, nx, ny, nz = s1.shape

    def fill(x, _):
        put_layer(pad, x + 1, lambda c, k: s1[c, x, k : k + CHUNK, :], lambda k: visc[x, k : k + CHUNK, :], ny)
        return 0

    lax.fori_loop(1, nx - 1, fill, 0)
    for side, ghost in enumerate((alo, ahi)):
        x = (nx - 1) * side
        put_layer(pad, x + 1, lambda c, k: edges[side, c, k : k + CHUNK, :], lambda k: visc[x, k : k + CHUNK, :], ny)
        outer = (nx + 1) * side
        pad[0:3, outer] = jnp.zeros((3,) + pad.shape[2:], F32)
        for k in range(0, ny, CHUNK):
            put(pad, 3, outer, TOP + k, ghost[3, k : k + CHUNK, :].astype(F32) * HALF, True)
    for ghost, row in ((ylo, TOP - 1), (yhi, TOP + ny)):
        value = ghost[3].astype(F32) * HALF
        for x in range(nx):
            put(pad, 3, x + 1, row, value[x : x + 1], True)
            for c in range(3):
                pad[c, x + 1, row : row + 1, :] = jnp.zeros((1, PADDED), F32)

    for side in range(2):
        sign = 1.0 if side else -1.0
        x, outer = 1 + (nx - 1) * side, (nx + 1) * side
        for k in range(TOP, TOP + ny, CHUNK):
            both = pad[3, x, k : k + CHUNK, :nz] + pad[3, outer, k : k + CHUNK, :nz]
            coef_x[side, k - TOP : k - TOP + CHUNK, :] = both - sign * HALF * pad[0, x, k : k + CHUNK, :nz]
        row, beyond = (TOP + ny - 1, TOP + ny) if side else (TOP, TOP - 1)
        for x in range(nx):
            both = pad[3, x + 1, row : row + 1, :nz] + pad[3, x + 1, beyond : beyond + 1, :nz]
            coef_y[side, x : x + 1, :] = both - sign * HALF * pad[1, x + 1, row : row + 1, :nz]

    def layer(x, side):
        for k in range(0, ny, CHUNK):
            new = update(pad, x + 1, TOP + k)
            for c in range(3):
                value = new[c][:, :nz]
                s2[c, x, k : k + CHUNK, :] = value.astype(BF16)
                if side is not None:
                    quasi[side, c, k : k + CHUNK, :] = value
                if k == 0:
                    quasi_rows[0, c, pl.ds(x, 1), :] = value[:1]
                    blocks[0, c, x] = value.astype(BF16)
                if k == ny - CHUNK:
                    quasi_rows[1, c, pl.ds(x, 1), :] = value[CHUNK - 1 :]
                    blocks[1, c, x] = value.astype(BF16)

    layer(0, 0)
    layer(nx - 1, 1)

    def middle(x, _):
        layer(x, None)
        return 0

    lax.fori_loop(1, nx - 1, middle, 0)

    taps = row_of.shape[0]
    rows = row_of[...]
    z = z_of[...]
    late = late_of[...]
    near = lax.broadcasted_iota(jnp.int32, (taps, nx * ny), 1)
    hot = jnp.where(near == rows, 1.0, 0.0).astype(BF16)
    middles = slice(ny, (nx - 1) * ny)
    for c in range(3):
        state[c, :ny, :] = edges[0, c]
        state[c, middles, :] = s1[c, 1 : nx - 1].reshape((nx - 2) * ny, nz)
        state[c, (nx - 1) * ny :, :] = edges[1, c]
    first = energies(hot, [state[c] for c in range(3)], z, nz)
    second = energies(hot, [s2[c].reshape(nx * ny, nz) for c in range(3)], z, nz)
    peaks[...] = jnp.maximum(first, jnp.where(late < 0, second, 0.0))
    column = lax.broadcasted_iota(jnp.int32, hot_late.shape, 1)
    hot_late[...] = jnp.where(column == late, 1.0, 0.0).astype(BF16)
    count = slots.shape[1]
    block = lax.broadcasted_iota(jnp.int32, (taps, count), 1)
    chosen = jnp.where(block == block_of[...], jnp.broadcast_to(slots[...], (taps, count)), 0.0)
    slot_of[...] = jnp.sum(chosen, axis=1, keepdims=True)


def second_edges(plo, phi, extra, quasi, coef_x, ylo, yhi, quasi_rows, coef_y, blocks, hot_late, z_of, slot_of, peaks, s2_in,
                 s2, best, layers, strips, late, sems):
    _, _, ny, nz = quasi.shape
    nx = quasi_rows.shape[2]
    ghosts_y = [[g[c].astype(F32) for c in range(3)] for g in (ylo, yhi)]
    copies = []
    added = [[coef_y[i] * ghosts_y[i][c] for c in range(3)] for i in range(2)]
    line = lax.broadcasted_iota(jnp.int32, (CHUNK, nz), 0)
    for side, ghost in enumerate((plo, phi)):
        x = (nx - 1) * side
        for c in range(3):
            for k in range(0, ny, CHUNK):
                part = slice(k, k + CHUNK)
                far = (ghost[c, part, :].astype(F32) + extra[side, c, part, :]).astype(BF16).astype(F32)
                value = quasi[side, c, part, :] + coef_x[side, part, :] * far
                if k == 0:
                    value = value + jnp.where(line == 0, jnp.broadcast_to(added[0][c][x : x + 1], line.shape), 0.0)
                if k == ny - CHUNK:
                    value = value + jnp.where(line == CHUNK - 1, jnp.broadcast_to(added[1][c][x : x + 1], line.shape), 0.0)
                value = value.astype(BF16)
                layers[side, c, part, :] = value
                late[c, side * ny + k : side * ny + k + CHUNK, :] = value
        copies.append(pltpu.make_async_copy(layers.at[side], s2.at[:, x], sems.at[side]))
        copies[-1].start()
    for c in range(3):
        fixed = [quasi_rows[i, c] + added[i][c] for i in range(2)]
        late[c, 2 * ny : 2 * ny + 2 * nx, :] = jnp.concatenate(fixed, axis=0).astype(BF16)
        for i in range(2):
            for x in range(1, nx - 1):
                fresh = jnp.broadcast_to(fixed[i][x : x + 1], line.shape)
                kept = blocks[i, c, x].astype(F32)
                strips[i, c, x - 1] = jnp.where(line == (CHUNK - 1) * i, fresh, kept).astype(BF16)
    for i in range(2):
        place = s2.at[:, 1 : nx - 1, (ny - CHUNK) * i : (ny - CHUNK) * i + CHUNK]
        copies.append(pltpu.make_async_copy(strips.at[i], place, sems.at[2 + i]))
        copies[-1].start()
    last = energies(hot_late[...], [late[c] for c in range(3)], z_of[...], nz)
    peak = jnp.maximum(peaks[...], last)
    slot = lax.broadcasted_iota(jnp.int32, (peak.shape[0], best.shape[1]), 1).astype(F32)
    best[...] = jnp.max(jnp.where(slot == slot_of[...], peak, 0.0), axis=0, keepdims=True)
    for copy in copies:
        copy.wait()


VM = pl.BlockSpec(memory_space=pltpu.VMEM)
HB = pl.BlockSpec(memory_space=pl.ANY)


def shape(dims, kind):
    return jax.ShapeDtypeStruct(dims, kind)


def body(velocity, viscosity, tap_cell, tap_block, block_slot):
    _, nx, ny, nz = velocity.shape
    taps = tap_cell.shape[1]
    count = block_slot.shape[0]
    padded = pltpu.VMEM((4, nx + 2, TOP + ny + 8, PADDED), F32)

    def perms(axis):
        peers = lax.axis_size(axis)
        up = [(i, (i + 1) % peers) for i in range(peers)]
        return up, [(j, i) for i, j in up]

    x_up, x_down = perms("gx")
    y_up, y_down = perms("gy")

    own_ylo = jnp.concatenate([velocity[:, :, 0], viscosity[None, :, 0]], axis=0)
    own_yhi = jnp.concatenate([velocity[:, :, ny - 1], viscosity[None, :, ny - 1]], axis=0)
    ylo = lax.ppermute(own_yhi, "gy", y_up)
    yhi = lax.ppermute(own_ylo, "gy", y_down)
    own_lo = jnp.concatenate([velocity[:, 0], viscosity[None, 0]], axis=0)
    own_hi = jnp.concatenate([velocity[:, nx - 1], viscosity[None, nx - 1]], axis=0)
    alo = lax.ppermute(own_hi, "gx", x_up)
    ahi = lax.ppermute(own_lo, "gx", x_down)

    cell = tap_cell[0]
    row_of = cell // nz
    z_of = (cell - row_of * nz)[:, None]
    tap_x, tap_y = row_of // ny, row_of % ny
    late_of = jnp.where(tap_y == 0, 2 * ny + tap_x, jnp.where(tap_y == ny - 1, 2 * ny + nx + tap_x, -1))
    late_of = jnp.where(tap_x == 0, tap_y, jnp.where(tap_x == nx - 1, ny + tap_y, late_of))[:, None]
    row_of = row_of[:, None]

    face = shape((3, ny, nz), BF16)
    s1, edge_lo, edge_hi, part, rows = pl.pallas_call(
        first_step,
        out_shape=(shape((3, nx, ny, nz), BF16), face, face, shape((2, 3, ny, nz), F32), shape((2, 3, nx, nz), F32)),
        in_specs=[VM] * 4,
        out_specs=[VM] * 5,
        scratch_shapes=[padded],
        compiler_params=pltpu.CompilerParams(vmem_limit_bytes=32 * 2**20),
        cost_estimate=pl.CostEstimate(flops=3 * 10**7, bytes_accessed=6 * 10**6, transcendentals=0),
        name="first_step",
    )(velocity, viscosity, ylo, yhi)
    plo = lax.ppermute(edge_hi, "gx", x_up)
    phi = lax.ppermute(edge_lo, "gx", x_down)

    yface = shape((3, nx, nz), BF16)
    edges, extra, face_lo, face_hi = pl.pallas_call(
        first_edges,
        out_shape=(shape((2, 3, ny, nz), BF16), shape((2, 3, ny, nz), F32), yface, yface),
        in_specs=[VM] * 6,
        out_specs=[VM] * 4,
        compiler_params=pltpu.CompilerParams(vmem_limit_bytes=16 * 2**20),
        cost_estimate=pl.CostEstimate(flops=3 * 10**6, bytes_accessed=3 * 10**6, transcendentals=0),
        name="first_edges",
    )(part, own_lo, own_hi, alo, ahi, rows)
    y2lo = lax.ppermute(face_hi, "gy", y_up)
    y2hi = lax.ppermute(face_lo, "gy", y_down)

    late_rows = 2 * ny + 2 * nx
    s2, quasi, quasi_rows, blocks, coef_x, coef_y, hot_late, slot_of, peaks = pl.pallas_call(
        second_step,
        out_shape=(
            shape((3, nx, ny, nz), BF16),
            shape((2, 3, ny, nz), F32),
            shape((2, 3, nx, nz), F32),
            shape((2, 3, nx, CHUNK, nz), BF16),
            shape((2, ny, nz), F32),
            shape((2, nx, nz), F32),
            shape((taps, late_rows), BF16),
            shape((taps, 1), F32),
            shape((taps, 1), F32),
        ),
        in_specs=[VM] * 12,
        out_specs=[VM] * 9,
        scratch_shapes=[padded, pltpu.VMEM((3, nx * ny, nz), BF16)],
        compiler_params=pltpu.CompilerParams(vmem_limit_bytes=32 * 2**20),
        cost_estimate=pl.CostEstimate(flops=3 * 10**7, bytes_accessed=8 * 10**6, transcendentals=0),
        name="second_step",
    )(s1, edges, viscosity, alo, ahi, ylo, yhi, row_of, z_of, late_of, tap_block[0][:, None], block_slot.astype(F32)[None])

    new_velocity, best = pl.pallas_call(
        second_edges,
        out_shape=(shape((3, nx, ny, nz), BF16), shape((1, count), F32)),
        in_specs=[VM] * 14 + [HB],
        out_specs=[HB, VM],
        scratch_shapes=[
            pltpu.VMEM((2, 3, ny, nz), BF16),
            pltpu.VMEM((2, 3, nx - 2, CHUNK, nz), BF16),
            pltpu.VMEM((3, late_rows, nz), BF16),
            pltpu.SemaphoreType.DMA((4,)),
        ],
        input_output_aliases={14: 0},
        compiler_params=pltpu.CompilerParams(vmem_limit_bytes=16 * 2**20),
        cost_estimate=pl.CostEstimate(flops=3 * 10**6, bytes_accessed=3 * 10**6, transcendentals=0),
        name="second_edges",
    )(plo, phi, extra, quasi, coef_x, y2lo, y2hi, quasi_rows, coef_y, blocks, hot_late, z_of, slot_of, peaks, s2)

    groups = lax.axis_size(("gx", "gy"))
    received = lax.all_to_all(best.reshape(groups, count // groups), ("gx", "gy"), split_axis=0, concat_axis=0, tiled=True)
    return new_velocity, jnp.max(received, axis=0)


def solution(mesh):
    placed = (
        P(None, "gx", "gy", None),
        P("gx", "gy", None),
        P(("gx", "gy"), None),
        P(("gx", "gy"), None),
        P(),
    )
    return jax.shard_map(
        body,
        mesh=mesh,
        in_specs=placed,
        out_specs=(P(None, "gx", "gy", None), P(("gx", "gy"))),
        check_vma=False,
    )
```

```python
import jax
import jax.numpy as jnp
from jax import lax
from jax.experimental import pallas as pl
from jax.experimental.pallas import tpu as pltpu
from jax.sharding import PartitionSpec as P

F32 = jnp.float32
BF16 = jnp.bfloat16
HALF = 0.15
TOP = 8
CHUNK = 16
PADDED = 640


def put(pad, field, x, row, value, low):
    rows, nz = value.shape
    pad[field, x, row : row + rows, :nz] = value
    lane = lax.broadcasted_iota(jnp.int32, (rows, PADDED - nz), 1)
    above = jnp.broadcast_to(value[:, nz - 1 : nz], lane.shape)
    below = jnp.broadcast_to(value[:, :1], lane.shape) if low else jnp.zeros(lane.shape, F32)
    pad[field, x, row : row + rows, nz:] = jnp.where(lane == PADDED - nz - 1, below, above)


def put_layer(pad, x, read_velocity, read_viscosity, ny):
    for k in range(0, ny, CHUNK):
        for c in range(3):
            put(pad, c, x, TOP + k, read_velocity(c, k).astype(F32), False)
        if read_viscosity is not None:
            put(pad, 3, x, TOP + k, read_viscosity(k).astype(F32) * HALF, True)


def update(pad, x, row):
    here = [pad[f, x, row : row + CHUNK, :] for f in range(4)]
    total = [here[0], here[1], here[2]]
    for d in range(3):
        drift = here[d] * HALF
        if d == 2:
            above = [pltpu.roll(v, PADDED - 1, 1) for v in here]
            high = above[3] + here[3]
            low = pltpu.roll(high, 1, 1)
            ups = [above[c] - here[c] for c in range(3)]
            downs = [pltpu.roll(u, 1, 1) for u in ups]
        else:
            if d == 0:
                above = [pad[f, x + 1, row : row + CHUNK, :] for f in range(4)]
                below = [pad[f, x - 1, row : row + CHUNK, :] for f in range(4)]
            else:
                above = [pad[f, x, row + 1 : row + 1 + CHUNK, :] for f in range(4)]
                below = [pad[f, x, row - 1 : row - 1 + CHUNK, :] for f in range(4)]
            high = above[3] + here[3]
            low = below[3] + here[3]
            ups = [above[c] - here[c] for c in range(3)]
            downs = [here[c] - below[c] for c in range(3)]
        plus = high - drift
        minus = low + drift
        for c in range(3):
            total[c] = total[c] + (plus * ups[c] - minus * downs[c])
    return total


def y_faces(vel, visc, ylo, yhi, block_v, block_n, sems):
    _, nx, ny, nz = vel.shape
    copies = []
    for i in range(2):
        rows = slice((ny - CHUNK) * i, (ny - CHUNK) * i + CHUNK)
        copies.append(pltpu.make_async_copy(vel.at[:, :, rows], block_v.at[i], sems.at[2 * i]))
        copies.append(pltpu.make_async_copy(visc.at[:, rows], block_n.at[i], sems.at[2 * i + 1]))
    for copy in copies:
        copy.start()
    line = lax.broadcasted_iota(jnp.int32, (nx, nz), 0)
    for i, out in enumerate((ylo, yhi)):
        copies[2 * i].wait()
        copies[2 * i + 1].wait()
        row = (CHUNK - 1) * i
        for f in range(4):
            total = jnp.zeros((nx, nz), F32)
            for x in range(nx):
                block = block_n[i, x] if f == 3 else block_v[i, f, x]
                one = block.astype(F32)[row : row + 1]
                total = jnp.where(line == x, jnp.broadcast_to(one, line.shape), total)
            out[f] = total.astype(BF16)


def x_faces(vel, visc, after, lo, hi, sems):
    nx = vel.shape[1]
    copies = []
    for i, out in enumerate((lo, hi)):
        x = (nx - 1) * i
        copies.append(pltpu.make_async_copy(vel.at[:, x], out.at[0:3], sems.at[2 * i]))
        copies.append(pltpu.make_async_copy(visc.at[x], out.at[3], sems.at[2 * i + 1]))
    for copy in copies:
        copy.start()
    for copy in copies:
        copy.wait()


def first_step(vel, visc, ylo, yhi, s1, part, edge_lo, edge_hi, rows, pad, inner, outer, sems):
    _, nx, ny, nz = vel.shape

    def fill(x, _):
        put_layer(pad, x + 1, lambda c, k: vel[c, x, k : k + CHUNK, :], lambda k: visc[x, k : k + CHUNK, :], ny)
        return 0

    lax.fori_loop(0, nx, fill, 0)
    for ghost, row in ((ylo, TOP - 1), (yhi, TOP + ny)):
        for f in range(4):
            value = ghost[f].astype(F32) * (HALF if f == 3 else 1.0)
            for x in range(nx):
                put(pad, f, x + 1, row, value[x : x + 1], f == 3)
    pad[:, 0] = pad[:, 1]
    pad[:, nx + 1] = pad[:, nx]

    def layer(x, side):
        for k in range(0, ny, CHUNK):
            new = update(pad, x + 1, TOP + k)
            for c in range(3):
                value = new[c][:, :nz]
                if side is None:
                    inner[c, x - 1, k : k + CHUNK, :] = value.astype(BF16)
                else:
                    (edge_lo, edge_hi)[side][c, k : k + CHUNK, :] = value.astype(BF16)
                    outer[side, c, k : k + CHUNK, :] = value
                if k == 0:
                    rows[0, c, pl.ds(x, 1), :] = value[:1]
                if k == ny - CHUNK:
                    rows[1, c, pl.ds(x, 1), :] = value[CHUNK - 1 :]

    layer(0, 0)
    layer(nx - 1, 1)
    edges_out = pltpu.make_async_copy(outer, part, sems.at[0])
    edges_out.start()

    def send(x):
        return pltpu.make_async_copy(inner.at[:, x - 1], s1.at[:, x - 1], sems.at[x])

    def middle(x, _):
        layer(x, None)
        send(x).start()
        return 0

    def finish(x, _):
        send(x).wait()
        return 0

    lax.fori_loop(1, nx - 1, middle, 0)
    lax.fori_loop(1, nx - 1, finish, 0)
    edges_out.wait()


def missing_terms(mine, far, sign):
    both = (mine[3] + far[3]) * HALF
    near_coef = both - sign * HALF * mine[0]
    far_coef = both + sign * HALF * far[0]
    gaps = [far[c] - mine[c] for c in range(3)]
    return [near_coef * g for g in gaps], [-far_coef * g for g in gaps]


def first_faces(rows, own_ylo, own_yhi, alo, ahi, face_lo, face_hi):
    _, _, nx, nz = rows.shape
    ny = alo.shape[1]
    line = lax.broadcasted_iota(jnp.int32, (nx, nz), 0)
    for i, (own, out) in enumerate(((own_ylo, face_lo), (own_yhi, face_hi))):
        values = [rows[i, c] for c in range(3)]
        for side, ghost in enumerate((alo, ahi)):
            x = (nx - 1) * side
            k = (ny - CHUNK) * i
            row = (CHUNK - 1) * i
            mine = [own[f].astype(F32)[x : x + 1] for f in range(4)]
            far = [ghost[f, k : k + CHUNK, :].astype(F32)[row : row + 1] for f in range(4)]
            terms, _ = missing_terms(mine, far, 1.0 if side else -1.0)
            for c in range(3):
                values[c] = values[c] + jnp.where(line == x, jnp.broadcast_to(terms[c], line.shape), 0.0)
        for c in range(3):
            out[c] = values[c].astype(BF16)


def energies(hot, states, z, nz):
    total = None
    for state in states:
        value = jnp.dot(hot, state, preferred_element_type=F32)
        total = value * value if total is None else total + value * value
    lane = lax.broadcasted_iota(jnp.int32, total.shape, 1)
    return jnp.max(jnp.where(lane == z, total, 0.0), axis=1, keepdims=True)


def second_step(s1, part, own_lo, own_hi, visc, alo, ahi, ylo, yhi, cells, tap_blocks, slots,
                s2, quasi, extra, quasi_rows, blocks, coef_x, coef_y, hot_late, z_of, slot_of, peaks, pad, state, outer, sems):
    _, nx, ny, nz = s2.shape
    edges_in = pltpu.make_async_copy(part, outer, sems.at[0])
    edges_in.start()

    def fetch(x):
        return pltpu.make_async_copy(s1.at[:, x - 1], state.at[:, x], sems.at[x])

    def begin(x, _):
        fetch(x).start()
        return 0

    lax.fori_loop(1, nx - 1, begin, 0)
    edges_in.wait()
    for side, (own, ghost) in enumerate(((own_lo, alo), (own_hi, ahi))):
        x = (nx - 1) * side
        beyond = (nx + 1) * side
        pad[0:3, beyond] = jnp.zeros((3,) + pad.shape[2:], F32)
        for k in range(0, ny, CHUNK):
            mine = [own[f, k : k + CHUNK, :].astype(F32) for f in range(4)]
            far = [ghost[f, k : k + CHUNK, :].astype(F32) for f in range(4)]
            terms, far_terms = missing_terms(mine, far, 1.0 if side else -1.0)
            put(pad, 3, beyond, TOP + k, far[3] * HALF, True)
            for c in range(3):
                state[c, x, k : k + CHUNK, :] = (outer[side, c, k : k + CHUNK, :] + terms[c]).astype(BF16)
                extra[side, c, k : k + CHUNK, :] = far_terms[c]

    def fill(x, _):
        put_layer(pad, x + 1, lambda c, k: state[c, x, k : k + CHUNK, :], lambda k: visc[x, k : k + CHUNK, :], ny)
        return 0

    def fetch_fill(x, _):
        fetch(x).wait()
        return fill(x, 0)

    fill(0, 0)
    fill(nx - 1, 0)
    lax.fori_loop(1, nx - 1, fetch_fill, 0)
    for ghost, row in ((ylo, TOP - 1), (yhi, TOP + ny)):
        value = ghost[3].astype(F32) * HALF
        for x in range(nx):
            put(pad, 3, x + 1, row, value[x : x + 1], True)
            for c in range(3):
                pad[c, x + 1, row : row + 1, :] = jnp.zeros((1, PADDED), F32)

    for side in range(2):
        sign = 1.0 if side else -1.0
        x, outer = 1 + (nx - 1) * side, (nx + 1) * side
        for k in range(TOP, TOP + ny, CHUNK):
            both = pad[3, x, k : k + CHUNK, :nz] + pad[3, outer, k : k + CHUNK, :nz]
            coef_x[side, k - TOP : k - TOP + CHUNK, :] = both - sign * HALF * pad[0, x, k : k + CHUNK, :nz]
        row, beyond = (TOP + ny - 1, TOP + ny) if side else (TOP, TOP - 1)
        for x in range(nx):
            both = pad[3, x + 1, row : row + 1, :nz] + pad[3, x + 1, beyond : beyond + 1, :nz]
            coef_y[side, x : x + 1, :] = both - sign * HALF * pad[1, x + 1, row : row + 1, :nz]

    def layer(x, side):
        for k in range(0, ny, CHUNK):
            new = update(pad, x + 1, TOP + k)
            for c in range(3):
                value = new[c][:, :nz]
                s2[c, x, k : k + CHUNK, :] = value.astype(BF16)
                if side is not None:
                    quasi[side, c, k : k + CHUNK, :] = value
                if k == 0:
                    quasi_rows[0, c, pl.ds(x, 1), :] = value[:1]
                    blocks[0, c, x] = value.astype(BF16)
                if k == ny - CHUNK:
                    quasi_rows[1, c, pl.ds(x, 1), :] = value[CHUNK - 1 :]
                    blocks[1, c, x] = value.astype(BF16)

    layer(0, 0)
    layer(nx - 1, 1)

    def middle(x, _):
        layer(x, None)
        return 0

    lax.fori_loop(1, nx - 1, middle, 0)

    taps = cells.shape[1]
    same = lax.broadcasted_iota(jnp.int32, (taps, taps), 0) == lax.broadcasted_iota(jnp.int32, (taps, taps), 1)

    def column_of(line):
        return jnp.sum(jnp.where(same, jnp.broadcast_to(line, same.shape), 0.0), axis=1, keepdims=True)

    cell = cells[...].astype(F32)
    line_rows = jnp.floor((cell + 0.5) * (1.0 / nz))
    line_x = jnp.floor((line_rows + 0.5) * (1.0 / ny))
    line_y = line_rows - line_x * ny
    line_late = jnp.where(line_y == 0, 2 * ny + line_x, jnp.where(line_y == ny - 1, 2 * ny + nx + line_x, -1.0))
    line_late = jnp.where(line_x == 0, line_y, jnp.where(line_x == nx - 1, ny + line_y, line_late))
    rows = column_of(line_rows).astype(jnp.int32)
    z = column_of(cell - line_rows * nz).astype(jnp.int32)
    late = column_of(line_late).astype(jnp.int32)
    z_of[...] = z
    near = lax.broadcasted_iota(jnp.int32, (taps, nx * ny), 1)
    hot = jnp.where(near == rows, 1.0, 0.0).astype(BF16)
    first = energies(hot, [state[c].reshape(nx * ny, nz) for c in range(3)], z, nz)
    second = energies(hot, [s2[c].reshape(nx * ny, nz) for c in range(3)], z, nz)
    peaks[...] = jnp.maximum(first, jnp.where(late < 0, second, 0.0))
    column = lax.broadcasted_iota(jnp.int32, hot_late.shape, 1)
    hot_late[...] = jnp.where(column == late, 1.0, 0.0).astype(BF16)
    count = slots.shape[1]
    block = lax.broadcasted_iota(jnp.int32, (taps, count), 1)
    wanted = column_of(tap_blocks[...].astype(F32)).astype(jnp.int32)
    chosen = jnp.where(block == wanted, jnp.broadcast_to(slots[...].astype(F32), (taps, count)), 0.0)
    slot_of[...] = jnp.sum(chosen, axis=1, keepdims=True)


def second_edges(plo, phi, extra, quasi, coef_x, ylo, yhi, quasi_rows, coef_y, blocks, hot_late, z_of, slot_of, peaks, s2_in,
                 s2, best, layers, strips, late, sems):
    _, _, ny, nz = quasi.shape
    nx = quasi_rows.shape[2]
    ghosts_y = [[g[c].astype(F32) for c in range(3)] for g in (ylo, yhi)]
    copies = []
    added = [[coef_y[i] * ghosts_y[i][c] for c in range(3)] for i in range(2)]
    line = lax.broadcasted_iota(jnp.int32, (CHUNK, nz), 0)
    for side, ghost in enumerate((plo, phi)):
        x = (nx - 1) * side
        for c in range(3):
            for k in range(0, ny, CHUNK):
                part = slice(k, k + CHUNK)
                far = (ghost[c, part, :].astype(F32) + extra[side, c, part, :]).astype(BF16).astype(F32)
                value = quasi[side, c, part, :] + coef_x[side, part, :] * far
                if k == 0:
                    value = value + jnp.where(line == 0, jnp.broadcast_to(added[0][c][x : x + 1], line.shape), 0.0)
                if k == ny - CHUNK:
                    value = value + jnp.where(line == CHUNK - 1, jnp.broadcast_to(added[1][c][x : x + 1], line.shape), 0.0)
                value = value.astype(BF16)
                layers[side, c, part, :] = value
                late[c, side * ny + k : side * ny + k + CHUNK, :] = value
        copies.append(pltpu.make_async_copy(layers.at[side], s2.at[:, x], sems.at[side]))
        copies[-1].start()
    for c in range(3):
        fixed = [quasi_rows[i, c] + added[i][c] for i in range(2)]
        late[c, 2 * ny : 2 * ny + 2 * nx, :] = jnp.concatenate(fixed, axis=0).astype(BF16)
        for i in range(2):
            for x in range(1, nx - 1):
                fresh = jnp.broadcast_to(fixed[i][x : x + 1], line.shape)
                kept = blocks[i, c, x].astype(F32)
                strips[i, c, x - 1] = jnp.where(line == (CHUNK - 1) * i, fresh, kept).astype(BF16)
    for i in range(2):
        place = s2.at[:, 1 : nx - 1, (ny - CHUNK) * i : (ny - CHUNK) * i + CHUNK]
        copies.append(pltpu.make_async_copy(strips.at[i], place, sems.at[2 + i]))
        copies[-1].start()
    last = energies(hot_late[...], [late[c] for c in range(3)], z_of[...], nz)
    peak = jnp.maximum(peaks[...], last)
    slot = lax.broadcasted_iota(jnp.int32, (peak.shape[0], best.shape[0] * best.shape[1]), 1).astype(F32)
    flat = jnp.max(jnp.where(slot == slot_of[...], peak, 0.0), axis=0, keepdims=True)
    owners, each = best.shape
    place = lax.broadcasted_iota(jnp.int32, (owners, owners * each), 1)
    first = each * lax.broadcasted_iota(jnp.int32, (owners, owners * each), 0)
    spread = jnp.broadcast_to(flat, place.shape)
    for j in range(each):
        best[:, j : j + 1] = jnp.max(jnp.where(place == first + j, spread, 0.0), axis=1, keepdims=True)
    for copy in copies:
        copy.wait()


VM = pl.BlockSpec(memory_space=pltpu.VMEM)
HB = pl.BlockSpec(memory_space=pltpu.HBM)


def shape(dims, kind):
    return jax.ShapeDtypeStruct(dims, kind)


def body(velocity, viscosity, tap_cell, tap_block, block_slot):
    _, nx, ny, nz = velocity.shape
    taps = tap_cell.shape[1]
    padded = pltpu.VMEM((4, nx + 2, TOP + ny + 8, PADDED), F32)

    def perms(axis):
        peers = lax.axis_size(axis)
        up = [(i, (i + 1) % peers) for i in range(peers)]
        return up, [(j, i) for i, j in up]

    x_up, x_down = perms("gx")
    y_up, y_down = perms("gy")

    own_ylo, own_yhi = pl.pallas_call(
        y_faces,
        out_shape=(shape((4, nx, nz), BF16),) * 2,
        in_specs=[HB] * 2,
        out_specs=[VM] * 2,
        scratch_shapes=[
            pltpu.VMEM((2, 3, nx, CHUNK, nz), BF16),
            pltpu.VMEM((2, nx, CHUNK, nz), BF16),
            pltpu.SemaphoreType.DMA((4,)),
        ],
        compiler_params=pltpu.CompilerParams(vmem_limit_bytes=60 * 2**20),
        name="y_faces",
    )(velocity, viscosity)
    ylo = lax.ppermute(own_yhi, "gy", y_up)
    yhi = lax.ppermute(own_ylo, "gy", y_down)
    own_lo, own_hi = pl.pallas_call(
        x_faces,
        out_shape=(shape((4, ny, nz), BF16),) * 2,
        in_specs=[HB] * 3,
        out_specs=[VM] * 2,
        scratch_shapes=[pltpu.SemaphoreType.DMA((4,))],
        compiler_params=pltpu.CompilerParams(vmem_limit_bytes=60 * 2**20),
        name="x_faces",
    )(velocity, viscosity, own_ylo)
    alo = lax.ppermute(own_hi, "gx", x_up)
    ahi = lax.ppermute(own_lo, "gx", x_down)

    face = shape((3, ny, nz), BF16)
    s1, part, edge_lo, edge_hi, rows = pl.pallas_call(
        first_step,
        out_shape=(shape((3, nx - 2, ny, nz), BF16), shape((2, 3, ny, nz), F32), face, face, shape((2, 3, nx, nz), F32)),
        in_specs=[VM] * 4,
        out_specs=[HB, HB, VM, VM, VM],
        scratch_shapes=[
            padded,
            pltpu.VMEM((3, nx - 2, ny, nz), BF16),
            pltpu.VMEM((2, 3, ny, nz), F32),
            pltpu.SemaphoreType.DMA((nx - 1,)),
        ],
        compiler_params=pltpu.CompilerParams(vmem_limit_bytes=28 * 2**20),
        cost_estimate=pl.CostEstimate(flops=10**10, bytes_accessed=6 * 10**6, transcendentals=0),
        name="first_step",
    )(velocity, viscosity, ylo, yhi)
    plo = lax.ppermute(edge_hi, "gx", x_up)
    phi = lax.ppermute(edge_lo, "gx", x_down)

    yface = shape((3, nx, nz), BF16)
    face_lo, face_hi = pl.pallas_call(
        first_faces,
        out_shape=(yface, yface),
        in_specs=[VM] * 5,
        out_specs=[VM] * 2,
        cost_estimate=pl.CostEstimate(flops=10**6, bytes_accessed=10**6, transcendentals=0),
        name="first_faces",
    )(rows, own_ylo, own_yhi, alo, ahi)
    y2lo = lax.ppermute(face_hi, "gy", y_up)
    y2hi = lax.ppermute(face_lo, "gy", y_down)

    groups = lax.axis_size(("gx", "gy"))
    each = block_slot.shape[0] // groups
    late_rows = 2 * ny + 2 * nx
    s2, quasi, extra, quasi_rows, blocks, coef_x, coef_y, hot_late, z_of, slot_of, peaks = pl.pallas_call(
        second_step,
        out_shape=(
            shape((3, nx, ny, nz), BF16),
            shape((2, 3, ny, nz), F32),
            shape((2, 3, ny, nz), F32),
            shape((2, 3, nx, nz), F32),
            shape((2, 3, nx, CHUNK, nz), BF16),
            shape((2, ny, nz), F32),
            shape((2, nx, nz), F32),
            shape((taps, late_rows), BF16),
            shape((taps, 1), jnp.int32),
            shape((taps, 1), F32),
            shape((taps, 1), F32),
        ),
        in_specs=[HB, HB] + [VM] * 10,
        out_specs=[VM] * 11,
        scratch_shapes=[
            padded,
            pltpu.VMEM((3, nx, ny, nz), BF16),
            pltpu.VMEM((2, 3, ny, nz), F32),
            pltpu.SemaphoreType.DMA((nx - 1,)),
        ],
        compiler_params=pltpu.CompilerParams(vmem_limit_bytes=32 * 2**20),
        cost_estimate=pl.CostEstimate(flops=3 * 10**7, bytes_accessed=8 * 10**6, transcendentals=0),
        name="second_step",
    )(s1, part, own_lo, own_hi, viscosity, alo, ahi, ylo, yhi, tap_cell, tap_block, block_slot[None])

    new_velocity, best = pl.pallas_call(
        second_edges,
        out_shape=(shape((3, nx, ny, nz), BF16), shape((groups, each), F32)),
        in_specs=[VM] * 14 + [HB],
        out_specs=[HB, VM],
        scratch_shapes=[
            pltpu.VMEM((2, 3, ny, nz), BF16),
            pltpu.VMEM((2, 3, nx - 2, CHUNK, nz), BF16),
            pltpu.VMEM((3, late_rows, nz), BF16),
            pltpu.SemaphoreType.DMA((4,)),
        ],
        input_output_aliases={14: 0},
        compiler_params=pltpu.CompilerParams(vmem_limit_bytes=16 * 2**20),
        cost_estimate=pl.CostEstimate(flops=3 * 10**6, bytes_accessed=3 * 10**6, transcendentals=0),
        name="second_edges",
    )(plo, phi, extra, quasi, coef_x, y2lo, y2hi, quasi_rows, coef_y, blocks, hot_late, z_of, slot_of, peaks, s2)

    received = lax.all_to_all(best, ("gx", "gy"), split_axis=0, concat_axis=0, tiled=True)
    return new_velocity, jnp.max(received, axis=0)


def solution(mesh):
    placed = (
        P(None, "gx", "gy", None),
        P("gx", "gy", None),
        P(("gx", "gy"), None),
        P(("gx", "gy"), None),
        P(),
    )
    return jax.shard_map(
        body,
        mesh=mesh,
        in_specs=placed,
        out_specs=(P(None, "gx", "gy", None), P(("gx", "gy"))),
        check_vma=False,
    )
```

```python
import jax
import jax.numpy as jnp
from jax import lax
from jax.experimental import pallas as pl
from jax.experimental.pallas import tpu as pltpu
from jax.sharding import PartitionSpec as P

F32 = jnp.float32
BF16 = jnp.bfloat16
HALF = 0.15
TOP = 8
CHUNK = 16
LANES = 128


def tiles_of(nz):
    return [(t, min(LANES, nz - t * LANES)) for t in range(-(-nz // LANES))]


def put(pad, field, x, row, value):
    rows, nz = value.shape
    for t, width in tiles_of(nz):
        piece = value[:, t * LANES : t * LANES + width]
        if width == LANES:
            pad[field, x, t, row : row + rows, :] = piece
        else:
            pad[field, x, t, row : row + rows, :width] = piece
            pad[field, x, t, row : row + rows, width:] = jnp.broadcast_to(piece[:, width - 1 :], (rows, LANES - width))


def put_layer(pad, x, read_velocity, read_viscosity, ny):
    for k in range(0, ny, CHUNK):
        for c in range(3):
            put(pad, c, x, TOP + k, read_velocity(c, k).astype(F32))
        put(pad, 3, x, TOP + k, read_viscosity(k).astype(F32) * HALF)


def update(pad, x, row, side, ghosts):
    tiles = pad.shape[2]
    lane = lax.broadcasted_iota(jnp.int32, (CHUNK, LANES), 1)

    def load(f, t, dx=0, dy=0):
        return pad[f, x + dx, t, row + dy : row + dy + CHUNK, :]

    result = []
    ahead = [pltpu.roll(load(f, 0), LANES - 1, 1) for f in range(4)]
    behind = None
    for t in range(tiles):
        here = [load(f, t) for f in range(4)]
        total = [here[0], here[1], here[2]]
        current = ahead
        if t + 1 < tiles:
            ahead = [pltpu.roll(load(f, t + 1), LANES - 1, 1) for f in range(4)]
            above_z = [jnp.where(lane == LANES - 1, ahead[f], current[f]) for f in range(4)]
        else:
            above_z = current
        turned = [pltpu.roll(here[f], 1, 1) for f in range(4)]
        if t:
            below_z = [jnp.where(lane == 0, behind[f], turned[f]) for f in range(4)]
        else:
            below_z = [jnp.where(lane == 0, here[f] if f == 3 else 0.0, turned[f]) for f in range(4)]
        behind = turned
        for d in range(3):
            drift = here[d] * HALF
            for up in (True, False):
                missing = d == 0 and side == (1 if up else 0)
                if missing and not ghosts:
                    continue
                if d == 2:
                    far = above_z if up else below_z
                else:
                    step = 1 if up else -1
                    dx, dy = (step, 0) if d == 0 else (0, step)
                    far = [None if missing and f < 3 else load(f, t, dx, dy) for f in range(4)]
                both = far[3] + here[3]
                coef = both - drift if up else both + drift
                for c in range(3):
                    gap = here[c] if far[c] is None else (here[c] - far[c])
                    total[c] = total[c] - coef * gap
        result.append((here, total))
    return result


def y_faces(vel, visc, ylo, yhi, block_v, block_n, sems):
    _, nx, ny, nz = vel.shape
    copies = []
    for i in range(2):
        rows = slice((ny - CHUNK) * i, (ny - CHUNK) * i + CHUNK)
        copies.append(pltpu.make_async_copy(vel.at[:, :, rows], block_v.at[i], sems.at[2 * i]))
        copies.append(pltpu.make_async_copy(visc.at[:, rows], block_n.at[i], sems.at[2 * i + 1]))
    for copy in copies:
        copy.start()
    line = lax.broadcasted_iota(jnp.int32, (nx, nz), 0)
    for i, out in enumerate((ylo, yhi)):
        copies[2 * i].wait()
        copies[2 * i + 1].wait()
        row = (CHUNK - 1) * i
        for f in range(4):
            total = jnp.zeros((nx, nz), F32)
            for x in range(nx):
                block = block_n[i, x] if f == 3 else block_v[i, f, x]
                one = block.astype(F32)[row : row + 1]
                total = jnp.where(line == x, jnp.broadcast_to(one, line.shape), total)
            out[f] = total.astype(BF16)


def x_faces(vel, visc, after, lo, hi, sems):
    nx = vel.shape[1]
    copies = []
    for i, out in enumerate((lo, hi)):
        x = (nx - 1) * i
        copies.append(pltpu.make_async_copy(vel.at[:, x], out.at[0:3], sems.at[2 * i]))
        copies.append(pltpu.make_async_copy(visc.at[x], out.at[3], sems.at[2 * i + 1]))
    for copy in copies:
        copy.start()
    for copy in copies:
        copy.wait()


def first_step(vel, visc, ylo, yhi, s1, part, edge_lo, edge_hi, rows, pad, inner, outer, lines, sems):
    _, nx, ny, nz = vel.shape

    def fill(x, _):
        put_layer(pad, x + 1, lambda c, k: vel[c, x, k : k + CHUNK, :], lambda k: visc[x, k : k + CHUNK, :], ny)
        return 0

    lax.fori_loop(0, nx, fill, 0)
    for ghost, row in ((ylo, TOP - 1), (yhi, TOP + ny)):
        for f in range(4):
            value = ghost[f].astype(F32) * (HALF if f == 3 else 1.0)
            for x in range(nx):
                put(pad, f, x + 1, row, value[x : x + 1])

    def layer(x, side):
        for k in range(0, ny, CHUNK):
            new = update(pad, x + 1, TOP + k, side, False)
            for t, width in tiles_of(nz):
                part = pl.ds(t * LANES, width)
                for c in range(3):
                    value = new[t][1][c][:, :width]
                    if side is None:
                        inner[c, x - 1, k : k + CHUNK, part] = value.astype(BF16)
                    else:
                        (edge_lo, edge_hi)[side][c, k : k + CHUNK, part] = value.astype(BF16)
                        outer[side, c, k : k + CHUNK, part] = value
                    if k == 0:
                        lines[0, c, x, :, part] = value[:1]
                    if k == ny - CHUNK:
                        lines[1, c, x, :, part] = value[CHUNK - 1 :]

    layer(0, 0)
    layer(nx - 1, 1)
    edges_out = pltpu.make_async_copy(outer, part, sems.at[0])
    edges_out.start()

    def send(x):
        return pltpu.make_async_copy(inner.at[:, x - 1], s1.at[:, x - 1], sems.at[x])

    def middle(x, _):
        layer(x, None)
        send(x).start()
        return 0

    def finish(x, _):
        send(x).wait()
        return 0

    lax.fori_loop(1, nx - 1, middle, 0)
    for i in range(2):
        for c in range(3):
            for x in range(nx):
                rows[i, c, x : x + 1, :] = lines[i, c, x]
    lax.fori_loop(1, nx - 1, finish, 0)
    edges_out.wait()


def missing_terms(mine, far, sign):
    both = (mine[3] + far[3]) * HALF
    near_coef = both - sign * HALF * mine[0]
    far_coef = both + sign * HALF * far[0]
    gaps = [far[c] - mine[c] for c in range(3)]
    return [near_coef * g for g in gaps], [-far_coef * g for g in gaps]


def first_faces(rows, own_ylo, own_yhi, alo, ahi, face_lo, face_hi):
    _, _, nx, nz = rows.shape
    ny = alo.shape[1]
    line = lax.broadcasted_iota(jnp.int32, (nx, nz), 0)
    for i, (own, out) in enumerate(((own_ylo, face_lo), (own_yhi, face_hi))):
        values = [rows[i, c] for c in range(3)]
        for side, ghost in enumerate((alo, ahi)):
            x = (nx - 1) * side
            k = (ny - CHUNK) * i
            row = (CHUNK - 1) * i
            mine = [own[f].astype(F32)[x : x + 1] for f in range(4)]
            far = [ghost[f, k : k + CHUNK, :].astype(F32)[row : row + 1] for f in range(4)]
            terms, _ = missing_terms(mine, far, 1.0 if side else -1.0)
            for c in range(3):
                values[c] = values[c] + jnp.where(line == x, jnp.broadcast_to(terms[c], line.shape), 0.0)
        for c in range(3):
            out[c] = values[c].astype(BF16)


def energies(hot, states, z, nz):
    total = None
    for state in states:
        value = jnp.dot(hot, state, preferred_element_type=F32)
        total = value * value if total is None else total + value * value
    lane = lax.broadcasted_iota(jnp.int32, total.shape, 1)
    return jnp.max(jnp.where(lane == z, total, 0.0), axis=1, keepdims=True)


def second_step(s1, part, own_lo, own_hi, visc, alo, ahi, ylo, yhi, cells, tap_blocks, slots,
                s2, quasi, extra, quasi_rows, blocks, coef_x, coef_y, hot_late, z_of, slot_of, peaks, pad, state, outer, strength, lines, sems):
    _, nx, ny, nz = s2.shape
    edges_in = pltpu.make_async_copy(part, outer, sems.at[0])
    edges_in.start()

    def fetch(x):
        return pltpu.make_async_copy(s1.at[:, x - 1], state.at[:, x], sems.at[x])

    def begin(x, _):
        fetch(x).start()
        return 0

    lax.fori_loop(1, nx - 1, begin, 0)
    edges_in.wait()
    for side, (own, ghost) in enumerate(((own_lo, alo), (own_hi, ahi))):
        x = (nx - 1) * side
        beyond = (nx + 1) * side
        for k in range(0, ny, CHUNK):
            mine = [own[f, k : k + CHUNK, :].astype(F32) for f in range(4)]
            far = [ghost[f, k : k + CHUNK, :].astype(F32) for f in range(4)]
            terms, far_terms = missing_terms(mine, far, 1.0 if side else -1.0)
            put(pad, 3, beyond, TOP + k, far[3] * HALF)
            for c in range(3):
                state[c, x, k : k + CHUNK, :] = (outer[side, c, k : k + CHUNK, :] + terms[c]).astype(BF16)
                extra[side, c, k : k + CHUNK, :] = far_terms[c]

    def fill(x, _):
        put_layer(pad, x + 1, lambda c, k: state[c, x, k : k + CHUNK, :], lambda k: visc[x, k : k + CHUNK, :], ny)
        return 0

    def fetch_fill(x, _):
        fetch(x).wait()
        return fill(x, 0)

    fill(0, 0)
    fill(nx - 1, 0)
    lax.fori_loop(1, nx - 1, fetch_fill, 0)
    for row in (0, TOP + ny):
        pad[0:3, 1 : nx + 1, :, row : row + TOP, :] = jnp.zeros((3, nx, pad.shape[2], TOP, LANES), F32)
    for ghost, row in ((ylo, TOP - 1), (yhi, TOP + ny)):
        value = ghost[3].astype(F32) * HALF
        for x in range(nx):
            put(pad, 3, x + 1, row, value[x : x + 1])

    for side in range(2):
        sign = 1.0 if side else -1.0
        x, beyond = 1 + (nx - 1) * side, (nx + 1) * side
        row, ghost_row = (TOP + ny - 1, TOP + ny) if side else (TOP, TOP - 1)
        for t, width in tiles_of(nz):
            part = pl.ds(t * LANES, width)
            for k in range(0, ny, CHUNK):
                rows = slice(TOP + k, TOP + k + CHUNK)
                both = pad[3, x, t, rows, :width] + pad[3, beyond, t, rows, :width]
                coef_x[side, k : k + CHUNK, part] = both - sign * HALF * pad[0, x, t, rows, :width]
            for y in range(nx):
                both = pad[3, y + 1, t, row : row + 1, :width] + pad[3, y + 1, t, ghost_row : ghost_row + 1, :width]
                coef_y[side, y : y + 1, part] = both - sign * HALF * pad[1, y + 1, t, row : row + 1, :width]

    line = lax.broadcasted_iota(jnp.int32, (CHUNK, LANES), 0)

    def layer(x, side):
        for k in range(0, ny, CHUNK):
            new = update(pad, x + 1, TOP + k, side, True)
            for t, width in tiles_of(nz):
                part = pl.ds(t * LANES, width)
                here, fresh = new[t]
                rounded = [v.astype(BF16) for v in fresh]
                energy = here[0] * here[0] + here[1] * here[1] + here[2] * here[2]
                if side is None:
                    again = [v.astype(F32) for v in rounded]
                    again = again[0] * again[0] + again[1] * again[1] + again[2] * again[2]
                    if k == 0:
                        again = jnp.where(line == 0, 0.0, again)
                    if k == ny - CHUNK:
                        again = jnp.where(line == CHUNK - 1, 0.0, again)
                    energy = jnp.maximum(energy, again)
                strength[pl.ds(x * ny + k, CHUNK), part] = energy[:, :width].astype(BF16)
                for c in range(3):
                    value = fresh[c][:, :width]
                    s2[c, x, k : k + CHUNK, part] = rounded[c][:, :width]
                    if side is not None:
                        quasi[side, c, k : k + CHUNK, part] = value
                    if k == 0:
                        lines[0, c, x, :, part] = value[:1]
                        blocks[0, c, x, :, part] = rounded[c][:, :width]
                    if k == ny - CHUNK:
                        lines[1, c, x, :, part] = value[CHUNK - 1 :]
                        blocks[1, c, x, :, part] = rounded[c][:, :width]

    layer(0, 0)
    layer(nx - 1, 1)

    def middle(x, _):
        layer(x, None)
        return 0

    lax.fori_loop(1, nx - 1, middle, 0)

    for i in range(2):
        for c in range(3):
            for x in range(nx):
                quasi_rows[i, c, x : x + 1, :] = lines[i, c, x]

    taps = cells.shape[1]
    same = lax.broadcasted_iota(jnp.int32, (taps, taps), 0) == lax.broadcasted_iota(jnp.int32, (taps, taps), 1)

    def column_of(line):
        return jnp.sum(jnp.where(same, jnp.broadcast_to(line, same.shape), 0.0), axis=1, keepdims=True)

    cell = cells[...].astype(F32)
    line_rows = jnp.floor((cell + 0.5) * (1.0 / nz))
    line_x = jnp.floor((line_rows + 0.5) * (1.0 / ny))
    line_y = line_rows - line_x * ny
    line_late = jnp.where(line_y == 0, 2 * ny + line_x, jnp.where(line_y == ny - 1, 2 * ny + nx + line_x, -1.0))
    line_late = jnp.where(line_x == 0, line_y, jnp.where(line_x == nx - 1, ny + line_y, line_late))
    rows = column_of(line_rows).astype(jnp.int32)
    z = column_of(cell - line_rows * nz).astype(jnp.int32)
    late = column_of(line_late).astype(jnp.int32)
    z_of[...] = z
    near = lax.broadcasted_iota(jnp.int32, (taps, nx * ny), 1)
    hot = jnp.where(near == rows, 1.0, 0.0).astype(BF16)
    picked = jnp.dot(hot, strength[...], preferred_element_type=F32)
    lane = lax.broadcasted_iota(jnp.int32, picked.shape, 1)
    peaks[...] = jnp.max(jnp.where(lane == z, picked, 0.0), axis=1, keepdims=True)
    column = lax.broadcasted_iota(jnp.int32, hot_late.shape, 1)
    hot_late[...] = jnp.where(column == late, 1.0, 0.0).astype(BF16)
    count = slots.shape[1]
    block = lax.broadcasted_iota(jnp.int32, (taps, count), 1)
    wanted = column_of(tap_blocks[...].astype(F32)).astype(jnp.int32)
    chosen = jnp.where(block == wanted, jnp.broadcast_to(slots[...].astype(F32), (taps, count)), 0.0)
    slot_of[...] = jnp.sum(chosen, axis=1, keepdims=True)


def second_edges(plo, phi, extra, quasi, coef_x, ylo, yhi, quasi_rows, coef_y, blocks, hot_late, z_of, slot_of, peaks, s2_in,
                 s2, best, layers, strips, late, sems):
    _, _, ny, nz = quasi.shape
    nx = quasi_rows.shape[2]
    ghosts_y = [[g[c].astype(F32) for c in range(3)] for g in (ylo, yhi)]
    copies = []
    added = [[coef_y[i] * ghosts_y[i][c] for c in range(3)] for i in range(2)]
    line = lax.broadcasted_iota(jnp.int32, (CHUNK, nz), 0)
    for side, ghost in enumerate((plo, phi)):
        x = (nx - 1) * side
        for c in range(3):
            for k in range(0, ny, CHUNK):
                part = slice(k, k + CHUNK)
                far = (ghost[c, part, :].astype(F32) + extra[side, c, part, :]).astype(BF16).astype(F32)
                value = quasi[side, c, part, :] + coef_x[side, part, :] * far
                if k == 0:
                    value = value + jnp.where(line == 0, jnp.broadcast_to(added[0][c][x : x + 1], line.shape), 0.0)
                if k == ny - CHUNK:
                    value = value + jnp.where(line == CHUNK - 1, jnp.broadcast_to(added[1][c][x : x + 1], line.shape), 0.0)
                value = value.astype(BF16)
                layers[side, c, part, :] = value
                late[c, side * ny + k : side * ny + k + CHUNK, :] = value
        copies.append(pltpu.make_async_copy(layers.at[side], s2.at[:, x], sems.at[side]))
        copies[-1].start()
    for c in range(3):
        fixed = [quasi_rows[i, c] + added[i][c] for i in range(2)]
        late[c, 2 * ny : 2 * ny + 2 * nx, :] = jnp.concatenate(fixed, axis=0).astype(BF16)
        for i in range(2):
            for x in range(1, nx - 1):
                fresh = jnp.broadcast_to(fixed[i][x : x + 1], line.shape)
                kept = blocks[i, c, x].astype(F32)
                strips[i, c, x - 1] = jnp.where(line == (CHUNK - 1) * i, fresh, kept).astype(BF16)
    for i in range(2):
        place = s2.at[:, 1 : nx - 1, (ny - CHUNK) * i : (ny - CHUNK) * i + CHUNK]
        copies.append(pltpu.make_async_copy(strips.at[i], place, sems.at[2 + i]))
        copies[-1].start()
    last = energies(hot_late[...], [late[c] for c in range(3)], z_of[...], nz)
    peak = jnp.maximum(peaks[...], last)
    slot = lax.broadcasted_iota(jnp.int32, (peak.shape[0], best.shape[0] * best.shape[1]), 1).astype(F32)
    flat = jnp.max(jnp.where(slot == slot_of[...], peak, 0.0), axis=0, keepdims=True)
    owners, each = best.shape
    place = lax.broadcasted_iota(jnp.int32, (owners, owners * each), 1)
    first = each * lax.broadcasted_iota(jnp.int32, (owners, owners * each), 0)
    spread = jnp.broadcast_to(flat, place.shape)
    for j in range(each):
        best[:, j : j + 1] = jnp.max(jnp.where(place == first + j, spread, 0.0), axis=1, keepdims=True)
    for copy in copies:
        copy.wait()


VM = pl.BlockSpec(memory_space=pltpu.VMEM)
HB = pl.BlockSpec(memory_space=pltpu.HBM)


def shape(dims, kind):
    return jax.ShapeDtypeStruct(dims, kind)


def body(velocity, viscosity, tap_cell, tap_block, block_slot):
    _, nx, ny, nz = velocity.shape
    taps = tap_cell.shape[1]
    padded = pltpu.VMEM((4, nx + 2, len(tiles_of(nz)), TOP + ny + 8, LANES), F32)

    def perms(axis):
        peers = lax.axis_size(axis)
        up = [(i, (i + 1) % peers) for i in range(peers)]
        return up, [(j, i) for i, j in up]

    x_up, x_down = perms("gx")
    y_up, y_down = perms("gy")

    own_ylo, own_yhi = pl.pallas_call(
        y_faces,
        out_shape=(shape((4, nx, nz), BF16),) * 2,
        in_specs=[HB] * 2,
        out_specs=[VM] * 2,
        scratch_shapes=[
            pltpu.VMEM((2, 3, nx, CHUNK, nz), BF16),
            pltpu.VMEM((2, nx, CHUNK, nz), BF16),
            pltpu.SemaphoreType.DMA((4,)),
        ],
        compiler_params=pltpu.CompilerParams(vmem_limit_bytes=60 * 2**20),
        name="y_faces",
    )(velocity, viscosity)
    ylo = lax.ppermute(own_yhi, "gy", y_up)
    yhi = lax.ppermute(own_ylo, "gy", y_down)
    own_lo, own_hi = pl.pallas_call(
        x_faces,
        out_shape=(shape((4, ny, nz), BF16),) * 2,
        in_specs=[HB] * 3,
        out_specs=[VM] * 2,
        scratch_shapes=[pltpu.SemaphoreType.DMA((4,))],
        compiler_params=pltpu.CompilerParams(vmem_limit_bytes=60 * 2**20),
        name="x_faces",
    )(velocity, viscosity, own_ylo)
    alo = lax.ppermute(own_hi, "gx", x_up)
    ahi = lax.ppermute(own_lo, "gx", x_down)

    face = shape((3, ny, nz), BF16)
    s1, part, edge_lo, edge_hi, rows = pl.pallas_call(
        first_step,
        out_shape=(shape((3, nx - 2, ny, nz), BF16), shape((2, 3, ny, nz), F32), face, face, shape((2, 3, nx, nz), F32)),
        in_specs=[VM] * 4,
        out_specs=[HB, HB, VM, VM, VM],
        scratch_shapes=[
            padded,
            pltpu.VMEM((3, nx - 2, ny, nz), BF16),
            pltpu.VMEM((2, 3, ny, nz), F32),
            pltpu.VMEM((2, 3, nx, 1, nz), F32),
            pltpu.SemaphoreType.DMA((nx - 1,)),
        ],
        compiler_params=pltpu.CompilerParams(vmem_limit_bytes=28 * 2**20),
        cost_estimate=pl.CostEstimate(flops=10**10, bytes_accessed=6 * 10**6, transcendentals=0),
        name="first_step",
    )(velocity, viscosity, ylo, yhi)
    plo = lax.ppermute(edge_hi, "gx", x_up)
    phi = lax.ppermute(edge_lo, "gx", x_down)

    yface = shape((3, nx, nz), BF16)
    face_lo, face_hi = pl.pallas_call(
        first_faces,
        out_shape=(yface, yface),
        in_specs=[VM] * 5,
        out_specs=[VM] * 2,
        compiler_params=pltpu.CompilerParams(vmem_limit_bytes=4 * 2**20),
        cost_estimate=pl.CostEstimate(flops=10**6, bytes_accessed=10**6, transcendentals=0),
        name="first_faces",
    )(rows, own_ylo, own_yhi, alo, ahi)
    y2lo = lax.ppermute(face_hi, "gy", y_up)
    y2hi = lax.ppermute(face_lo, "gy", y_down)

    groups = lax.axis_size(("gx", "gy"))
    each = block_slot.shape[0] // groups
    late_rows = 2 * ny + 2 * nx
    s2, quasi, extra, quasi_rows, blocks, coef_x, coef_y, hot_late, z_of, slot_of, peaks = pl.pallas_call(
        second_step,
        out_shape=(
            shape((3, nx, ny, nz), BF16),
            shape((2, 3, ny, nz), F32),
            shape((2, 3, ny, nz), F32),
            shape((2, 3, nx, nz), F32),
            shape((2, 3, nx, CHUNK, nz), BF16),
            shape((2, ny, nz), F32),
            shape((2, nx, nz), F32),
            shape((taps, late_rows), BF16),
            shape((taps, 1), jnp.int32),
            shape((taps, 1), F32),
            shape((taps, 1), F32),
        ),
        in_specs=[HB, HB] + [VM] * 10,
        out_specs=[VM] * 11,
        scratch_shapes=[
            padded,
            pltpu.VMEM((3, nx, ny, nz), BF16),
            pltpu.VMEM((2, 3, ny, nz), F32),
            pltpu.VMEM((nx * ny, nz), BF16),
            pltpu.VMEM((2, 3, nx, 1, nz), F32),
            pltpu.SemaphoreType.DMA((nx - 1,)),
        ],
        compiler_params=pltpu.CompilerParams(vmem_limit_bytes=32 * 2**20),
        cost_estimate=pl.CostEstimate(flops=3 * 10**7, bytes_accessed=8 * 10**6, transcendentals=0),
        name="second_step",
    )(s1, part, own_lo, own_hi, viscosity, alo, ahi, ylo, yhi, tap_cell, tap_block, block_slot[None])

    new_velocity, best = pl.pallas_call(
        second_edges,
        out_shape=(shape((3, nx, ny, nz), BF16), shape((groups, each), F32)),
        in_specs=[VM] * 14 + [HB],
        out_specs=[HB, VM],
        scratch_shapes=[
            pltpu.VMEM((2, 3, ny, nz), BF16),
            pltpu.VMEM((2, 3, nx - 2, CHUNK, nz), BF16),
            pltpu.VMEM((3, late_rows, nz), BF16),
            pltpu.SemaphoreType.DMA((4,)),
        ],
        input_output_aliases={14: 0},
        compiler_params=pltpu.CompilerParams(vmem_limit_bytes=16 * 2**20),
        cost_estimate=pl.CostEstimate(flops=3 * 10**6, bytes_accessed=3 * 10**6, transcendentals=0),
        name="second_edges",
    )(plo, phi, extra, quasi, coef_x, y2lo, y2hi, quasi_rows, coef_y, blocks, hot_late, z_of, slot_of, peaks, s2)

    received = lax.all_to_all(best, ("gx", "gy"), split_axis=0, concat_axis=0, tiled=True)
    return new_velocity, jnp.max(received, axis=0)


def solution(mesh):
    placed = (
        P(None, "gx", "gy", None),
        P("gx", "gy", None),
        P(("gx", "gy"), None),
        P(("gx", "gy"), None),
        P(),
    )
    return jax.shard_map(
        body,
        mesh=mesh,
        in_specs=placed,
        out_specs=(P(None, "gx", "gy", None), P(("gx", "gy"))),
        check_vma=False,
    )
```

```python
import jax
import jax.numpy as jnp
from jax import lax
from jax.experimental import pallas as pl
from jax.experimental.pallas import tpu as pltpu
from jax.sharding import PartitionSpec as P

F32 = jnp.float32
BF16 = jnp.bfloat16
HALF = 0.15
TOP = 8
CHUNK = 16
LANES = 128


def tiles_of(nz):
    return [(t, min(LANES, nz - t * LANES)) for t in range(-(-nz // LANES))]


def put(pad, index, row, value):
    rows, nz = value.shape
    for t, width in tiles_of(nz):
        pad[(*index, t, slice(row, row + rows), slice(0, width))] = value[:, t * LANES : t * LANES + width]


def update(load, packed, side, ghosts, nz):
    lane = lax.broadcasted_iota(jnp.int32, (CHUNK, LANES), 1)

    def tile(t, width):
        values = [packed(f, pl.ds(t * LANES, width)) for f in range(4)]
        if width < LANES:
            values = [jnp.concatenate([v, jnp.zeros((CHUNK, LANES - width), BF16)], axis=1) for v in values]
        return values

    def wide(values):
        return [v.astype(F32) * HALF if f == 3 else v.astype(F32) for f, v in enumerate(values)]

    spans = tiles_of(nz)
    result = []
    own = tile(*spans[0])
    ahead = [pltpu.roll(v, LANES - 1, 1) for v in own]
    behind = None
    for t, width in spans:
        here = [load(f, t, 0, 0) for f in range(4)]
        current, now = ahead, own
        if t + 1 < len(spans):
            own = tile(*spans[t + 1])
            ahead = [pltpu.roll(v, LANES - 1, 1) for v in own]
            beyond = ahead
        else:
            beyond = now
        above_z = wide([jnp.where(lane == width - 1, beyond[f], current[f]) for f in range(4)])
        turned = [pltpu.roll(v, 1, 1) for v in now]
        if t:
            before = behind
        else:
            before = [jnp.zeros((CHUNK, LANES), BF16)] * 3 + [now[3]]
        below_z = wide([jnp.where(lane == 0, before[f], turned[f]) for f in range(4)])
        behind = turned
        weight = None
        terms = [[], [], []]
        for d in range(3):
            drift = here[d] * HALF
            for up in (True, False):
                missing = d == 0 and side == (1 if up else 0)
                if missing and not ghosts:
                    weight = drift if up else weight - drift
                    continue
                if d == 2:
                    far = above_z if up else below_z
                else:
                    step = 1 if up else -1
                    dx, dy = (step, 0) if d == 0 else (0, step)
                    far = [None if missing and f < 3 else load(f, t, dx, dy) for f in range(4)]
                both = far[3] + here[3]
                weight = both if weight is None else weight + both
                if far[0] is not None:
                    coef = both - drift if up else both + drift
                    for c in range(3):
                        terms[c].append(coef * far[c])
        weight = 1.0 - weight
        total = [here[c] * weight for c in range(3)]
        for c in range(3):
            for term in terms[c]:
                total[c] = total[c] + term
        result.append((here, total))
    return result


def x_face(vel, visc, lo, sems):
    copies = [pltpu.make_async_copy(vel.at[:, 0], lo.at[0:3], sems.at[0]), pltpu.make_async_copy(visc.at[0], lo.at[3], sems.at[1])]
    for copy in copies:
        copy.start()
    for copy in copies:
        copy.wait()


def other_faces(vel, visc, after, ylo, yhi, hi):
    _, nx, ny, nz = vel.shape
    hi[0:3] = vel[:, nx - 1]
    hi[3] = visc[nx - 1]
    line = lax.broadcasted_iota(jnp.int32, (nx, nz), 0)
    for i, out in enumerate((ylo, yhi)):
        rows = slice((ny - CHUNK) * i, (ny - CHUNK) * i + CHUNK)
        row = (CHUNK - 1) * i
        for f in range(4):
            total = jnp.zeros((nx, nz), F32)
            for x in range(nx):
                block = visc[x, rows] if f == 3 else vel[f, x, rows]
                one = block.astype(F32)[row : row + 1]
                total = jnp.where(line == x, jnp.broadcast_to(one, line.shape), total)
            out[f] = total.astype(BF16)


def first_step(vel, visc, ylo, yhi, next_pad, nu_pad, packed, edge_lo, edge_hi, rows, pad, lines):
    _, nx, ny, nz = vel.shape
    tiles = len(tiles_of(nz))

    def fill(x, _):
        for k in range(0, ny, CHUNK):
            for c in range(3):
                put(pad, (c, x), TOP + k, vel[c, x, k : k + CHUNK, :].astype(F32))
            put(nu_pad, (x,), TOP + k, visc[x, k : k + CHUNK, :].astype(F32) * HALF)
        return 0

    lax.fori_loop(0, nx, fill, 0)
    for ghost, row in ((ylo, TOP - 1), (yhi, TOP + ny)):
        for f in range(4):
            value = ghost[f].astype(F32) * (HALF if f == 3 else 1.0)
            for x in range(nx):
                if f == 3:
                    put(nu_pad, (x,), row, value[x : x + 1])
                else:
                    put(pad, (f, x), row, value[x : x + 1])
    for row in (0, TOP + ny):
        next_pad[:, :, :, row : row + TOP, :] = jnp.zeros((3, nx, tiles, TOP, LANES), F32)

    def layer(x, side):
        for k in range(0, ny, CHUNK):

            def load(f, t, dx, dy):
                window = pl.ds(TOP + k + dy, CHUNK)
                return nu_pad[x + dx, t, window, :] if f == 3 else pad[f, x + dx, t, window, :]

            def bits(f, part):
                return visc[x, k : k + CHUNK, part] if f == 3 else vel[f, x, k : k + CHUNK, part]

            new = update(load, bits, side, False, nz)
            for t, width in tiles_of(nz):
                part = pl.ds(t * LANES, width)
                for c in range(3):
                    value = new[t][1][c]
                    rounded = value.astype(BF16)
                    if k == 0:
                        lines[0, c, x, :, part] = value[:1, :width]
                    if k == ny - CHUNK:
                        lines[1, c, x, :, part] = value[CHUNK - 1 :, :width]
                    if side is not None:
                        (edge_lo, edge_hi)[side][c, k : k + CHUNK, part] = rounded[:, :width]
                    else:
                        value = rounded.astype(F32)
                        packed[c, x - 1, k : k + CHUNK, part] = rounded[:, :width]
                    next_pad[c, x, t, TOP + k : TOP + k + CHUNK, :] = value

    layer(0, 0)
    layer(nx - 1, 1)

    def middle(x, _):
        layer(x, None)
        return 0

    lax.fori_loop(1, nx - 1, middle, 0)
    for i in range(2):
        for c in range(3):
            for x in range(nx):
                rows[i, c, x : x + 1, :] = lines[i, c, x]


def missing_terms(mine, far, sign):
    both = (mine[3] + far[3]) * HALF
    near_coef = both - sign * HALF * mine[0]
    far_coef = both + sign * HALF * far[0]
    gaps = [far[c] - mine[c] for c in range(3)]
    return [near_coef * g for g in gaps], [-far_coef * g for g in gaps]


def first_faces(rows, own_ylo, own_yhi, alo, ahi, after, face_lo, face_hi):
    _, _, nx, nz = rows.shape
    ny = alo.shape[1]
    line = lax.broadcasted_iota(jnp.int32, (nx, nz), 0)
    for i, (own, out) in enumerate(((own_ylo, face_lo), (own_yhi, face_hi))):
        values = [rows[i, c] for c in range(3)]
        for side, ghost in enumerate((alo, ahi)):
            x = (nx - 1) * side
            k = (ny - CHUNK) * i
            row = (CHUNK - 1) * i
            mine = [own[f].astype(F32)[x : x + 1] for f in range(4)]
            far = [ghost[f, k : k + CHUNK, :].astype(F32)[row : row + 1] for f in range(4)]
            terms, _ = missing_terms(mine, far, 1.0 if side else -1.0)
            for c in range(3):
                values[c] = values[c] + jnp.where(line == x, jnp.broadcast_to(terms[c], line.shape), 0.0)
        for c in range(3):
            out[c] = values[c].astype(BF16)


def emit(new, nz, k, ny, store, strength, strength_row, blocks, lines, both_steps):
    line = lax.broadcasted_iota(jnp.int32, (CHUNK, LANES), 0)
    for t, width in tiles_of(nz):
        part = pl.ds(t * LANES, width)
        here, fresh = new[t]
        rounded = [v.astype(BF16) for v in fresh]
        energy = here[0] * here[0] + here[1] * here[1] + here[2] * here[2]
        if both_steps:
            again = [v.astype(F32) for v in rounded]
            again = again[0] * again[0] + again[1] * again[1] + again[2] * again[2]
            if k == 0:
                again = jnp.where(line == 0, 0.0, again)
            if k == ny - CHUNK:
                again = jnp.where(line == CHUNK - 1, 0.0, again)
            energy = jnp.maximum(energy, again)
        strength[pl.ds(strength_row, CHUNK), part] = energy[:, :width].astype(BF16)
        for c in range(3):
            store(c, part, fresh[c][:, :width], rounded[c][:, :width])
            if k == 0:
                lines(0, c, part, fresh[c][:1, :width])
                blocks(0, c, part, rounded[c][:, :width])
            if k == ny - CHUNK:
                lines(1, c, part, fresh[c][CHUNK - 1 :, :width])
                blocks(1, c, part, rounded[c][:, :width])


def gather(hot, states, z):
    total = None
    for state in states:
        value = jnp.dot(hot, state, preferred_element_type=F32)
        if len(states) > 1:
            value = value * value
        total = value if total is None else total + value
    lane = lax.broadcasted_iota(jnp.int32, total.shape, 1)
    return jnp.max(jnp.where(lane == z, total, 0.0), axis=1, keepdims=True)


def second_middle(pad, nu_pad, packed, visc, after, cells, tap_blocks, slots,
                  s2, blocks, rows, hot_outer, hot_late, z_of, slot_of, peaks, inner, strength, lines, sem):
    _, nx, tiles, _, _ = pad.shape
    ny, nz = inner.shape[2:]

    def layer(x, _):
        for k in range(0, ny, CHUNK):

            def load(f, t, dx, dy):
                window = pl.ds(TOP + k + dy, CHUNK)
                return nu_pad[x + dx, t, window, :] if f == 3 else pad[f, x + dx, t, window, :]

            def store(c, part, value, rounded):
                inner[c, x - 2, k : k + CHUNK, part] = rounded

            def put_block(i, c, part, rounded):
                blocks[i, c, x - 2, :, part] = rounded

            def put_line(i, c, part, value):
                lines[i, c, x - 2, :, part] = value

            def bits(f, part):
                return visc[x, k : k + CHUNK, part] if f == 3 else packed[f, x - 1, k : k + CHUNK, part]

            new = update(load, bits, None, True, nz)
            emit(new, nz, k, ny, store, strength, (x - 2) * ny + k, put_block, put_line, True)
        return 0

    lax.fori_loop(2, nx - 2, layer, 0)
    copy = pltpu.make_async_copy(inner, s2.at[:, 2 : nx - 2], sem)
    copy.start()
    for i in range(2):
        for c in range(3):
            for x in range(nx - 4):
                rows[i, c, x : x + 1, :] = lines[i, c, x]

    taps = cells.shape[1]
    same = lax.broadcasted_iota(jnp.int32, (taps, taps), 0) == lax.broadcasted_iota(jnp.int32, (taps, taps), 1)

    def column_of(line):
        return jnp.sum(jnp.where(same, jnp.broadcast_to(line, same.shape), 0.0), axis=1, keepdims=True)

    def one_hot(column, width):
        position = lax.broadcasted_iota(jnp.int32, (taps, width), 1)
        return jnp.where(position == column.astype(jnp.int32), 1.0, 0.0).astype(BF16)

    cell = cells[...].astype(F32)
    line_rows = jnp.floor((cell + 0.5) * (1.0 / nz))
    line_x = jnp.floor((line_rows + 0.5) * (1.0 / ny))
    line_y = line_rows - line_x * ny
    line_late = jnp.where(line_y == 0, 2 * ny + line_x, jnp.where(line_y == ny - 1, 2 * ny + nx + line_x, -1.0))
    line_late = jnp.where(line_x == 0, line_y, jnp.where(line_x == nx - 1, ny + line_y, line_late))
    row = column_of(line_rows)
    middle = row - 2 * ny
    outer = jnp.where(row < 2 * ny, row, jnp.where(row < (nx - 2) * ny, -1.0, row - (nx - 4) * ny))
    z = column_of(cell - line_rows * nz).astype(jnp.int32)
    z_of[...] = z
    hot_outer[...] = one_hot(outer, hot_outer.shape[1])
    hot_late[...] = one_hot(column_of(line_late), hot_late.shape[1])
    peaks[...] = gather(one_hot(middle, (nx - 4) * ny), [strength[...]], z)
    count = slots.shape[1]
    block = lax.broadcasted_iota(jnp.int32, (taps, count), 1)
    wanted = column_of(tap_blocks[...].astype(F32)).astype(jnp.int32)
    chosen = jnp.where(block == wanted, jnp.broadcast_to(slots[...].astype(F32), (taps, count)), 0.0)
    slot_of[...] = jnp.sum(chosen, axis=1, keepdims=True)
    copy.wait()


def second_outer(pad, nu_pad, packed, visc, own_lo, own_hi, alo, ahi, hot_outer, z_of, peaks_in, s2_in,
                 s2, quasi, extra, rows, blocks, coef_x, coef_y, peaks, edge, edge_bits, ghost_nu, inner, strength, lines, sems):
    _, nx, tiles, _, _ = pad.shape
    ny, nz = inner.shape[3:]
    for side, (own, ghost) in enumerate(((own_lo, alo), (own_hi, ahi))):
        x = (nx - 1) * side
        for k in range(0, ny, CHUNK):
            mine = [own[f, k : k + CHUNK, :].astype(F32) for f in range(4)]
            far = [ghost[f, k : k + CHUNK, :].astype(F32) for f in range(4)]
            terms, far_terms = missing_terms(mine, far, 1.0 if side else -1.0)
            put(ghost_nu, (side,), TOP + k, far[3] * HALF)
            for c in range(3):
                extra[side, c, k : k + CHUNK, :] = far_terms[c]
                for t, width in tiles_of(nz):
                    part = slice(t * LANES, t * LANES + width)
                    window = slice(TOP + k, TOP + k + CHUNK)
                    value = (pad[c, x, t, window, :width] + terms[c][:, part]).astype(BF16)
                    edge[c, side, t, window, :width] = value.astype(F32)
                    edge_bits[c, side, k : k + CHUNK, part] = value
    for row in (0, TOP + ny):
        edge[:, :, :, row : row + TOP, :] = jnp.zeros((3, 2, tiles, TOP, LANES), F32)

    def read(f, x, t, window):
        if f == 3:
            return ghost_nu[0, t, window, :] if x < 0 else ghost_nu[1, t, window, :] if x == nx else nu_pad[x, t, window, :]
        return edge[f, 0, t, window, :] if x == 0 else edge[f, 1, t, window, :] if x == nx - 1 else pad[f, x, t, window, :]

    for side in range(2):
        sign = 1.0 if side else -1.0
        x, beyond = (nx - 1) * side, nx if side else -1
        row, ghost_row = (TOP + ny - 1, TOP + ny) if side else (TOP, TOP - 1)
        for t, width in tiles_of(nz):
            part = pl.ds(t * LANES, width)
            for k in range(0, ny, CHUNK):
                window = slice(TOP + k, TOP + k + CHUNK)
                both = read(3, x, t, window) + read(3, beyond, t, window)
                coef_x[side, k : k + CHUNK, part] = (both - sign * HALF * read(0, x, t, window))[:, :width]
            for y in range(nx):
                window, other = slice(row, row + 1), slice(ghost_row, ghost_row + 1)
                both = read(3, y, t, window) + read(3, y, t, other)
                coef_y[side, y : y + 1, part] = (both - sign * HALF * read(1, y, t, window))[:, :width]

    for side in range(2):
        for j in range(2):
            x = (nx - 1 - j) * side + j * (1 - side)
            for k in range(0, ny, CHUNK):

                def load(f, t, dx, dy):
                    return read(f, x + dx, t, slice(TOP + k + dy, TOP + k + dy + CHUNK))

                def store(c, part, value, rounded):
                    if j:
                        inner[side, c, 0, k : k + CHUNK, part] = rounded
                    else:
                        quasi[side, c, k : k + CHUNK, part] = value

                def put_block(i, c, part, rounded):
                    if j:
                        blocks[i, c, side, :, part] = rounded

                def put_line(i, c, part, value):
                    lines[i, c, 2 * side + j, :, part] = value

                def bits(f, part):
                    if f == 3:
                        return visc[x, k : k + CHUNK, part]
                    return packed[f, x - 1, k : k + CHUNK, part] if j else edge_bits[f, side, k : k + CHUNK, part]

                new = update(load, bits, None if j else side, True, nz)
                strength_row = (2 * side + (1 - j if side else j)) * ny + k
                emit(new, nz, k, ny, store, strength, strength_row, put_block, put_line, j == 1)
    copies = [pltpu.make_async_copy(inner.at[i], s2.at[:, pl.ds(1 + (nx - 3) * i, 1)], sems.at[i]) for i in range(2)]
    for copy in copies:
        copy.start()
    for i in range(2):
        for c in range(3):
            for j in range(4):
                rows[i, c, j : j + 1, :] = lines[i, c, j]
    peaks[...] = jnp.maximum(peaks_in[...], gather(hot_outer[...], [strength[...]], z_of[...]))
    for copy in copies:
        copy.wait()


def second_edges(plo, phi, extra, quasi, coef_x, ylo, yhi, rows_middle, rows_outer, coef_y, blocks_middle, blocks_outer,
                 hot_late, z_of, slot_of, peaks, s2_in, s2, best, layers, strips, late, sems):
    _, _, ny, nz = quasi.shape
    nx = ylo.shape[1]
    copies = []
    added = [[coef_y[i] * g[c].astype(F32) for c in range(3)] for i, g in enumerate((ylo, yhi))]
    line = lax.broadcasted_iota(jnp.int32, (CHUNK, nz), 0)
    for side, ghost in enumerate((plo, phi)):
        x = (nx - 1) * side
        for c in range(3):
            for k in range(0, ny, CHUNK):
                part = slice(k, k + CHUNK)
                far = (ghost[c, part, :].astype(F32) + extra[side, c, part, :]).astype(BF16).astype(F32)
                value = quasi[side, c, part, :] + coef_x[side, part, :] * far
                if k == 0:
                    value = value + jnp.where(line == 0, jnp.broadcast_to(added[0][c][x : x + 1], line.shape), 0.0)
                if k == ny - CHUNK:
                    value = value + jnp.where(line == CHUNK - 1, jnp.broadcast_to(added[1][c][x : x + 1], line.shape), 0.0)
                value = value.astype(BF16)
                layers[side, c, part, :] = value
                late[c, side * ny + k : side * ny + k + CHUNK, :] = value
        copies.append(pltpu.make_async_copy(layers.at[side], s2.at[:, x], sems.at[side]))
        copies[-1].start()
    for c in range(3):
        fixed = []
        for i in range(2):
            outer = rows_outer[i, c]
            base = jnp.concatenate([outer[:2], rows_middle[i, c], outer[3:4], outer[2:3]], axis=0)
            fixed.append(base + added[i][c])
        late[c, 2 * ny : 2 * ny + 2 * nx, :] = jnp.concatenate(fixed, axis=0).astype(BF16)
        for i in range(2):
            for x in range(1, nx - 1):
                fresh = jnp.broadcast_to(fixed[i][x : x + 1], line.shape)
                outer = x == 1 or x == nx - 2
                kept = blocks_outer[i, c, 0 if x == 1 else 1] if outer else blocks_middle[i, c, x - 2]
                strips[i, c, x - 1] = jnp.where(line == (CHUNK - 1) * i, fresh, kept.astype(F32)).astype(BF16)
    for i in range(2):
        place = s2.at[:, 1 : nx - 1, (ny - CHUNK) * i : (ny - CHUNK) * i + CHUNK]
        copies.append(pltpu.make_async_copy(strips.at[i], place, sems.at[2 + i]))
        copies[-1].start()
    last = gather(hot_late[...], [late[c] for c in range(3)], z_of[...])
    peak = jnp.maximum(peaks[...], last)
    slot = lax.broadcasted_iota(jnp.int32, (peak.shape[0], best.shape[0] * best.shape[1]), 1).astype(F32)
    flat = jnp.max(jnp.where(slot == slot_of[...], peak, 0.0), axis=0, keepdims=True)
    owners, each = best.shape
    place = lax.broadcasted_iota(jnp.int32, (owners, owners * each), 1)
    first = each * lax.broadcasted_iota(jnp.int32, (owners, owners * each), 0)
    wide = jnp.broadcast_to(flat, place.shape)
    for j in range(each):
        best[:, j : j + 1] = jnp.max(jnp.where(place == first + j, wide, 0.0), axis=1, keepdims=True)
    for copy in copies:
        copy.wait()


VM = pl.BlockSpec(memory_space=pltpu.VMEM)
HB = pl.BlockSpec(memory_space=pltpu.HBM)


def shape(dims, kind):
    return jax.ShapeDtypeStruct(dims, kind)


FIRST = 10**6
MIDDLE = 8 * 10**9


def call(kernel, ins, outs, scratch, mib, flops, **others):
    return pl.pallas_call(
        kernel,
        out_shape=tuple(o for o, _ in outs),
        in_specs=ins,
        out_specs=[spec for _, spec in outs],
        scratch_shapes=scratch,
        compiler_params=pltpu.CompilerParams(vmem_limit_bytes=mib * 2**20),
        cost_estimate=pl.CostEstimate(flops=flops, bytes_accessed=10**6, transcendentals=0),
        name=kernel.__name__,
        **others,
    )


def body(velocity, viscosity, tap_cell, tap_block, block_slot):
    _, nx, ny, nz = velocity.shape
    taps = tap_cell.shape[1]
    tiles = len(tiles_of(nz))
    tall = TOP + ny + 8
    groups = lax.axis_size(("gx", "gy"))
    each = block_slot.shape[0] // groups
    late_rows = 2 * ny + 2 * nx

    def perms(axis):
        peers = lax.axis_size(axis)
        up = [(i, (i + 1) % peers) for i in range(peers)]
        return up, [(j, i) for i, j in up]

    x_up, x_down = perms("gx")
    y_up, y_down = perms("gy")

    yface = (shape((4, nx, nz), BF16), VM)
    xface = (shape((4, ny, nz), BF16), VM)
    (own_lo,) = call(x_face, [HB] * 2, [xface], [pltpu.SemaphoreType.DMA((2,))], 60, 10**6)(velocity, viscosity)
    ahi = lax.ppermute(own_lo, "gx", x_down)
    own_ylo, own_yhi, own_hi = call(other_faces, [VM] * 2 + [HB], [yface, yface, xface], [], 8, 10**6)(velocity, viscosity, own_lo)
    ylo = lax.ppermute(own_yhi, "gy", y_up)
    yhi = lax.ppermute(own_ylo, "gy", y_down)
    alo = lax.ppermute(own_hi, "gx", x_up)

    face = (shape((3, ny, nz), BF16), VM)
    outs = [
        (shape((3, nx, tiles, tall, LANES), F32), VM),
        (shape((nx, tiles, tall, LANES), F32), VM),
        (shape((3, nx - 2, ny, nz), BF16), VM),
        face,
        face,
        (shape((2, 3, nx, nz), F32), VM),
    ]
    scratch = [pltpu.VMEM((3, nx, tiles, tall, LANES), F32), pltpu.VMEM((2, 3, nx, 1, nz), F32)]
    pad, nu_pad, packed, edge_lo, edge_hi, rows = call(first_step, [VM] * 4, outs, scratch, 28, FIRST)(velocity, viscosity, ylo, yhi)
    plo = lax.ppermute(edge_hi, "gx", x_up)
    phi = lax.ppermute(edge_lo, "gx", x_down)

    whole = (shape((3, nx, ny, nz), BF16), HB)
    column = (shape((taps, 1), F32), VM)
    outs = [
        whole,
        (shape((2, 3, nx - 4, CHUNK, nz), BF16), VM),
        (shape((2, 3, nx - 4, nz), F32), VM),
        (shape((taps, 4 * ny), BF16), VM),
        (shape((taps, late_rows), BF16), VM),
        (shape((taps, 1), jnp.int32), VM),
        column,
        column,
    ]
    scratch = [
        pltpu.VMEM((3, nx - 4, ny, nz), BF16),
        pltpu.VMEM(((nx - 4) * ny, nz), BF16),
        pltpu.VMEM((2, 3, nx - 4, 1, nz), F32),
        pltpu.SemaphoreType.DMA,
    ]
    s2, blocks_middle, rows_middle, hot_outer, hot_late, z_of, slot_of, peaks = call(
        second_middle, [VM] * 4 + [HB] + [VM] * 3, outs, scratch, 28, MIDDLE
    )(pad, nu_pad, packed, viscosity, ahi, tap_cell, tap_block, block_slot[None])

    yface = (shape((3, nx, nz), BF16), VM)
    face_lo, face_hi = call(first_faces, [VM] * 6, [yface, yface], [], 4, 10**6)(rows, own_ylo, own_yhi, alo, ahi, slot_of)
    y2lo = lax.ppermute(face_hi, "gy", y_up)
    y2hi = lax.ppermute(face_lo, "gy", y_down)

    outs = [
        whole,
        (shape((2, 3, ny, nz), F32), VM),
        (shape((2, 3, ny, nz), F32), VM),
        (shape((2, 3, 4, nz), F32), VM),
        (shape((2, 3, 2, CHUNK, nz), BF16), VM),
        (shape((2, ny, nz), F32), VM),
        (shape((2, nx, nz), F32), VM),
        column,
    ]
    scratch = [
        pltpu.VMEM((3, 2, tiles, tall, LANES), F32),
        pltpu.VMEM((3, 2, ny, nz), BF16),
        pltpu.VMEM((2, tiles, tall, LANES), F32),
        pltpu.VMEM((2, 3, 1, ny, nz), BF16),
        pltpu.VMEM((4 * ny, nz), BF16),
        pltpu.VMEM((2, 3, 4, 1, nz), F32),
        pltpu.SemaphoreType.DMA((2,)),
    ]
    s2, quasi, extra, rows_outer, blocks_outer, coef_x, coef_y, peaks = call(
        second_outer, [VM] * 11 + [HB], outs, scratch, 28, 10**6, input_output_aliases={11: 0}
    )(pad, nu_pad, packed, viscosity, own_lo, own_hi, alo, ahi, hot_outer, z_of, peaks, s2)

    scratch = [
        pltpu.VMEM((2, 3, ny, nz), BF16),
        pltpu.VMEM((2, 3, nx - 2, CHUNK, nz), BF16),
        pltpu.VMEM((3, late_rows, nz), BF16),
        pltpu.SemaphoreType.DMA((4,)),
    ]
    new_velocity, best = call(
        second_edges, [VM] * 16 + [HB], [whole, (shape((groups, each), F32), VM)], scratch, 16, 10**6, input_output_aliases={16: 0}
    )(plo, phi, extra, quasi, coef_x, y2lo, y2hi, rows_middle, rows_outer, coef_y, blocks_middle, blocks_outer,
      hot_late, z_of, slot_of, peaks, s2)

    received = lax.all_to_all(best, ("gx", "gy"), split_axis=0, concat_axis=0, tiled=True)
    return new_velocity, jnp.max(received, axis=0)


def solution(mesh):
    placed = (
        P(None, "gx", "gy", None),
        P("gx", "gy", None),
        P(("gx", "gy"), None),
        P(("gx", "gy"), None),
        P(),
    )
    return jax.shard_map(
        body,
        mesh=mesh,
        in_specs=placed,
        out_specs=(P(None, "gx", "gy", None), P(("gx", "gy"))),
        check_vma=False,
    )
```

```python
import jax
import jax.numpy as jnp
from jax import lax
from jax.experimental import pallas as pl
from jax.experimental.pallas import tpu as pltpu
from jax.sharding import PartitionSpec as P

F32 = jnp.float32
BF16 = jnp.bfloat16
HALF = 0.15
TOP = 8
CHUNK = 16
LANES = 128


def tiles_of(nz):
    return [(t, min(LANES, nz - t * LANES)) for t in range(-(-nz // LANES))]


def put(pad, index, row, value):
    rows, nz = value.shape
    for t, width in tiles_of(nz):
        pad[(*index, t, slice(row, row + rows), slice(0, width))] = value[:, t * LANES : t * LANES + width]


def update(load, packed, side, ghosts, nz):
    lane = lax.broadcasted_iota(jnp.int32, (CHUNK, LANES), 1)

    def tile(t, width):
        values = [packed(f, pl.ds(t * LANES, width)) for f in range(4)]
        if width < LANES:
            values = [jnp.concatenate([v, jnp.zeros((CHUNK, LANES - width), BF16)], axis=1) for v in values]
        return values

    def wide(values):
        return [v.astype(F32) * HALF if f == 3 else v.astype(F32) for f, v in enumerate(values)]

    spans = tiles_of(nz)
    result = []
    own = tile(*spans[0])
    ahead = [pltpu.roll(v, LANES - 1, 1) for v in own]
    behind = None
    for t, width in spans:
        here = [load(f, t, 0, 0) for f in range(4)]
        current, now = ahead, own
        if t + 1 < len(spans):
            own = tile(*spans[t + 1])
            ahead = [pltpu.roll(v, LANES - 1, 1) for v in own]
            beyond = ahead
        else:
            beyond = now
        above_z = wide([jnp.where(lane == width - 1, beyond[f], current[f]) for f in range(4)])
        turned = [pltpu.roll(v, 1, 1) for v in now]
        if t:
            before = behind
        else:
            before = [jnp.zeros((CHUNK, LANES), BF16)] * 3 + [now[3]]
        below_z = wide([jnp.where(lane == 0, before[f], turned[f]) for f in range(4)])
        behind = turned
        weight = None
        terms = [[], [], []]
        for d in range(3):
            drift = here[d] * HALF
            for up in (True, False):
                missing = d == 0 and side == (1 if up else 0)
                if missing and not ghosts:
                    weight = drift if up else weight - drift
                    continue
                if d == 2:
                    far = above_z if up else below_z
                else:
                    step = 1 if up else -1
                    dx, dy = (step, 0) if d == 0 else (0, step)
                    far = [None if missing and f < 3 else load(f, t, dx, dy) for f in range(4)]
                both = far[3] + here[3]
                weight = both if weight is None else weight + both
                if far[0] is not None:
                    coef = both - drift if up else both + drift
                    for c in range(3):
                        terms[c].append(coef * far[c])
        weight = 1.0 - weight
        total = [here[c] * weight for c in range(3)]
        for c in range(3):
            for term in terms[c]:
                total[c] = total[c] + term
        result.append((here, total))
    return result


def x_face(vel, visc, lo, sems):
    copies = [pltpu.make_async_copy(vel.at[:, 0], lo.at[0:3], sems.at[0]), pltpu.make_async_copy(visc.at[0], lo.at[3], sems.at[1])]
    for copy in copies:
        copy.start()
    for copy in copies:
        copy.wait()


def other_faces(vel, visc, after, ylo, yhi, hi):
    _, nx, ny, nz = vel.shape
    hi[0:3] = vel[:, nx - 1]
    hi[3] = visc[nx - 1]
    line = lax.broadcasted_iota(jnp.int32, (nx, nz), 0)
    for i, out in enumerate((ylo, yhi)):
        rows = slice((ny - CHUNK) * i, (ny - CHUNK) * i + CHUNK)
        row = (CHUNK - 1) * i
        for f in range(4):
            total = jnp.zeros((nx, nz), F32)
            for x in range(nx):
                block = visc[x, rows] if f == 3 else vel[f, x, rows]
                one = block.astype(F32)[row : row + 1]
                total = jnp.where(line == x, jnp.broadcast_to(one, line.shape), total)
            out[f] = total.astype(BF16)


def first_step(vel, visc, ylo, yhi, next_pad, nu_pad, packed, edge_lo, edge_hi, rows, pad, lines):
    _, nx, ny, nz = vel.shape
    tiles = len(tiles_of(nz))

    def fill(x, _):
        for k in range(0, ny, CHUNK):
            for c in range(3):
                put(pad, (c, x), TOP + k, vel[c, x, k : k + CHUNK, :].astype(F32))
            put(nu_pad, (x,), TOP + k, visc[x, k : k + CHUNK, :].astype(F32) * HALF)
        return 0

    lax.fori_loop(0, nx, fill, 0)
    for ghost, row in ((ylo, TOP - 1), (yhi, TOP + ny)):
        for f in range(4):
            value = ghost[f].astype(F32) * (HALF if f == 3 else 1.0)
            for x in range(nx):
                if f == 3:
                    put(nu_pad, (x,), row, value[x : x + 1])
                else:
                    put(pad, (f, x), row, value[x : x + 1])
    for row in (0, TOP + ny):
        next_pad[:, :, :, row : row + TOP, :] = jnp.zeros((3, nx, tiles, TOP, LANES), F32)

    def layer(x, side):
        for k in range(0, ny, CHUNK):

            def load(f, t, dx, dy):
                window = pl.ds(TOP + k + dy, CHUNK)
                return nu_pad[x + dx, t, window, :] if f == 3 else pad[f, x + dx, t, window, :]

            def bits(f, part):
                return visc[x, k : k + CHUNK, part] if f == 3 else vel[f, x, k : k + CHUNK, part]

            new = update(load, bits, side, False, nz)
            for t, width in tiles_of(nz):
                part = pl.ds(t * LANES, width)
                for c in range(3):
                    value = new[t][1][c]
                    rounded = value.astype(BF16)
                    if k == 0:
                        lines[0, c, x, :, part] = value[:1, :width]
                    if k == ny - CHUNK:
                        lines[1, c, x, :, part] = value[CHUNK - 1 :, :width]
                    if side is not None:
                        (edge_lo, edge_hi)[side][c, k : k + CHUNK, part] = rounded[:, :width]
                    else:
                        value = rounded.astype(F32)
                        packed[c, x - 1, k : k + CHUNK, part] = rounded[:, :width]
                    next_pad[c, x, t, TOP + k : TOP + k + CHUNK, :] = value

    layer(0, 0)
    layer(nx - 1, 1)

    def middle(x, _):
        layer(x, None)
        return 0

    lax.fori_loop(1, nx - 1, middle, 0)
    for i in range(2):
        for c in range(3):
            for x in range(nx):
                rows[i, c, x : x + 1, :] = lines[i, c, x]


def missing_terms(mine, far, sign):
    both = (mine[3] + far[3]) * HALF
    near_coef = both - sign * HALF * mine[0]
    far_coef = both + sign * HALF * far[0]
    gaps = [far[c] - mine[c] for c in range(3)]
    return [near_coef * g for g in gaps], [-far_coef * g for g in gaps]


def first_faces(rows, own_ylo, own_yhi, alo, ahi, after, face_lo, face_hi):
    _, _, nx, nz = rows.shape
    ny = alo.shape[1]
    line = lax.broadcasted_iota(jnp.int32, (nx, nz), 0)
    for i, (own, out) in enumerate(((own_ylo, face_lo), (own_yhi, face_hi))):
        values = [rows[i, c] for c in range(3)]
        for side, ghost in enumerate((alo, ahi)):
            x = (nx - 1) * side
            k = (ny - CHUNK) * i
            row = (CHUNK - 1) * i
            mine = [own[f].astype(F32)[x : x + 1] for f in range(4)]
            far = [ghost[f, k : k + CHUNK, :].astype(F32)[row : row + 1] for f in range(4)]
            terms, _ = missing_terms(mine, far, 1.0 if side else -1.0)
            for c in range(3):
                values[c] = values[c] + jnp.where(line == x, jnp.broadcast_to(terms[c], line.shape), 0.0)
        for c in range(3):
            out[c] = values[c].astype(BF16)


def emit(new, nz, k, ny, store, strength, strength_row, blocks, lines, both_steps):
    line = lax.broadcasted_iota(jnp.int32, (CHUNK, LANES), 0)
    for t, width in tiles_of(nz):
        part = pl.ds(t * LANES, width)
        here, fresh = new[t]
        rounded = [v.astype(BF16) for v in fresh]
        energy = here[0] * here[0] + here[1] * here[1] + here[2] * here[2]
        if both_steps:
            again = [v.astype(F32) for v in rounded]
            again = again[0] * again[0] + again[1] * again[1] + again[2] * again[2]
            if k == 0:
                again = jnp.where(line == 0, 0.0, again)
            if k == ny - CHUNK:
                again = jnp.where(line == CHUNK - 1, 0.0, again)
            energy = jnp.maximum(energy, again)
        strength[pl.ds(strength_row, CHUNK), part] = energy[:, :width].astype(BF16)
        for c in range(3):
            store(c, part, fresh[c][:, :width], rounded[c][:, :width])
            if k == 0:
                lines(0, c, part, fresh[c][:1, :width])
                blocks(0, c, part, rounded[c][:, :width])
            if k == ny - CHUNK:
                lines(1, c, part, fresh[c][CHUNK - 1 :, :width])
                blocks(1, c, part, rounded[c][:, :width])


def gather(hot, states, z):
    total = None
    for state in states:
        value = jnp.dot(hot, state, preferred_element_type=F32)
        if len(states) > 1:
            value = value * value
        total = value if total is None else total + value
    lane = lax.broadcasted_iota(jnp.int32, total.shape, 1)
    return jnp.max(jnp.where(lane == z, total, 0.0), axis=1, keepdims=True)


def second_middle(pad, nu_pad, packed, visc, after, cells, tap_blocks, slots,
                  s2, blocks, rows, hot_outer, hot_late, z_of, slot_of, peaks, inner, strength, lines, sem):
    _, nx, tiles, _, _ = pad.shape
    ny, nz = inner.shape[2:]

    def layer(x, _):
        for k in range(0, ny, CHUNK):

            def load(f, t, dx, dy):
                window = pl.ds(TOP + k + dy, CHUNK)
                return nu_pad[x + dx, t, window, :] if f == 3 else pad[f, x + dx, t, window, :]

            def store(c, part, value, rounded):
                inner[c, x - 2, k : k + CHUNK, part] = rounded

            def put_block(i, c, part, rounded):
                blocks[i, c, x - 2, :, part] = rounded

            def put_line(i, c, part, value):
                lines[i, c, x - 2, :, part] = value

            def bits(f, part):
                return visc[x, k : k + CHUNK, part] if f == 3 else packed[f, x - 1, k : k + CHUNK, part]

            new = update(load, bits, None, True, nz)
            emit(new, nz, k, ny, store, strength, (x - 2) * ny + k, put_block, put_line, True)
        return 0

    lax.fori_loop(2, nx - 2, layer, 0)
    copy = pltpu.make_async_copy(inner, s2.at[:, 2 : nx - 2], sem)
    copy.start()
    for i in range(2):
        for c in range(3):
            for x in range(nx - 4):
                rows[i, c, x : x + 1, :] = lines[i, c, x]

    taps = cells.shape[1]
    same = lax.broadcasted_iota(jnp.int32, (taps, taps), 0) == lax.broadcasted_iota(jnp.int32, (taps, taps), 1)

    def column_of(line):
        return jnp.sum(jnp.where(same, jnp.broadcast_to(line, same.shape), 0.0), axis=1, keepdims=True)

    def one_hot(column, width):
        position = lax.broadcasted_iota(jnp.int32, (taps, width), 1)
        return jnp.where(position == column.astype(jnp.int32), 1.0, 0.0).astype(BF16)

    cell = cells[...].astype(F32)
    line_rows = jnp.floor((cell + 0.5) * (1.0 / nz))
    line_x = jnp.floor((line_rows + 0.5) * (1.0 / ny))
    line_y = line_rows - line_x * ny
    line_late = jnp.where(line_y == 0, 2 * ny + line_x, jnp.where(line_y == ny - 1, 2 * ny + nx + line_x, -1.0))
    line_late = jnp.where(line_x == 0, line_y, jnp.where(line_x == nx - 1, ny + line_y, line_late))
    row = column_of(line_rows)
    middle = row - 2 * ny
    outer = jnp.where(row < 2 * ny, row, jnp.where(row < (nx - 2) * ny, -1.0, row - (nx - 4) * ny))
    z = column_of(cell - line_rows * nz).astype(jnp.int32)
    z_of[...] = z
    hot_outer[...] = one_hot(outer, hot_outer.shape[1])
    hot_late[...] = one_hot(column_of(line_late), hot_late.shape[1])
    peaks[...] = gather(one_hot(middle, (nx - 4) * ny), [strength[...]], z)
    count = slots.shape[1]
    block = lax.broadcasted_iota(jnp.int32, (taps, count), 1)
    wanted = column_of(tap_blocks[...].astype(F32)).astype(jnp.int32)
    chosen = jnp.where(block == wanted, jnp.broadcast_to(slots[...].astype(F32), (taps, count)), 0.0)
    slot_of[...] = jnp.sum(chosen, axis=1, keepdims=True)
    copy.wait()


def second_outer(pad, nu_pad, packed, visc, own_lo, own_hi, alo, ahi, hot_outer, z_of, peaks_in, s2_in,
                 s2, quasi, extra, rows, blocks, coef_x, coef_y, peaks, edge, edge_bits, ghost_nu, inner, strength, lines, sems):
    _, nx, tiles, _, _ = pad.shape
    ny, nz = inner.shape[3:]
    for side, (own, ghost) in enumerate(((own_lo, alo), (own_hi, ahi))):
        x = (nx - 1) * side
        for k in range(0, ny, CHUNK):
            mine = [own[f, k : k + CHUNK, :].astype(F32) for f in range(4)]
            far = [ghost[f, k : k + CHUNK, :].astype(F32) for f in range(4)]
            terms, far_terms = missing_terms(mine, far, 1.0 if side else -1.0)
            put(ghost_nu, (side,), TOP + k, far[3] * HALF)
            for c in range(3):
                extra[side, c, k : k + CHUNK, :] = far_terms[c]
                for t, width in tiles_of(nz):
                    part = slice(t * LANES, t * LANES + width)
                    window = slice(TOP + k, TOP + k + CHUNK)
                    value = (pad[c, x, t, window, :width] + terms[c][:, part]).astype(BF16)
                    edge[c, side, t, window, :width] = value.astype(F32)
                    edge_bits[c, side, k : k + CHUNK, part] = value
    for row in (0, TOP + ny):
        edge[:, :, :, row : row + TOP, :] = jnp.zeros((3, 2, tiles, TOP, LANES), F32)

    def read(f, x, t, window):
        if f == 3:
            return ghost_nu[0, t, window, :] if x < 0 else ghost_nu[1, t, window, :] if x == nx else nu_pad[x, t, window, :]
        return edge[f, 0, t, window, :] if x == 0 else edge[f, 1, t, window, :] if x == nx - 1 else pad[f, x, t, window, :]

    for side in range(2):
        sign = 1.0 if side else -1.0
        x, beyond = (nx - 1) * side, nx if side else -1
        row, ghost_row = (TOP + ny - 1, TOP + ny) if side else (TOP, TOP - 1)
        for t, width in tiles_of(nz):
            part = pl.ds(t * LANES, width)
            for k in range(0, ny, CHUNK):
                window = slice(TOP + k, TOP + k + CHUNK)
                both = read(3, x, t, window) + read(3, beyond, t, window)
                coef_x[side, k : k + CHUNK, part] = (both - sign * HALF * read(0, x, t, window))[:, :width]
            for y in range(nx):
                window, other = slice(row, row + 1), slice(ghost_row, ghost_row + 1)
                both = read(3, y, t, window) + read(3, y, t, other)
                coef_y[side, y : y + 1, part] = (both - sign * HALF * read(1, y, t, window))[:, :width]

    for side in range(2):
        for j in range(2):
            x = (nx - 1 - j) * side + j * (1 - side)
            for k in range(0, ny, CHUNK):

                def load(f, t, dx, dy):
                    return read(f, x + dx, t, slice(TOP + k + dy, TOP + k + dy + CHUNK))

                def store(c, part, value, rounded):
                    if j:
                        inner[side, c, 0, k : k + CHUNK, part] = rounded
                    else:
                        quasi[side, c, k : k + CHUNK, part] = value

                def put_block(i, c, part, rounded):
                    if j:
                        blocks[i, c, side, :, part] = rounded

                def put_line(i, c, part, value):
                    lines[i, c, 2 * side + j, :, part] = value

                def bits(f, part):
                    if f == 3:
                        return visc[x, k : k + CHUNK, part]
                    return packed[f, x - 1, k : k + CHUNK, part] if j else edge_bits[f, side, k : k + CHUNK, part]

                new = update(load, bits, None if j else side, True, nz)
                strength_row = (2 * side + (1 - j if side else j)) * ny + k
                emit(new, nz, k, ny, store, strength, strength_row, put_block, put_line, j == 1)
    copies = [pltpu.make_async_copy(inner.at[i], s2.at[:, pl.ds(1 + (nx - 3) * i, 1)], sems.at[i]) for i in range(2)]
    for copy in copies:
        copy.start()
    for i in range(2):
        for c in range(3):
            for j in range(4):
                rows[i, c, j : j + 1, :] = lines[i, c, j]
    peaks[...] = jnp.maximum(peaks_in[...], gather(hot_outer[...], [strength[...]], z_of[...]))
    for copy in copies:
        copy.wait()


def second_edges(plo, phi, extra, quasi, coef_x, ylo, yhi, rows_middle, rows_outer, coef_y, blocks_middle, blocks_outer,
                 hot_late, z_of, slot_of, peaks, s2_in, s2, best, layers, strips, late, sems):
    _, _, ny, nz = quasi.shape
    nx = ylo.shape[1]
    copies = []
    added = [[coef_y[i] * g[c].astype(F32) for c in range(3)] for i, g in enumerate((ylo, yhi))]
    line = lax.broadcasted_iota(jnp.int32, (CHUNK, nz), 0)
    for side, ghost in enumerate((plo, phi)):
        x = (nx - 1) * side
        for c in range(3):
            for k in range(0, ny, CHUNK):
                part = slice(k, k + CHUNK)
                far = (ghost[c, part, :].astype(F32) + extra[side, c, part, :]).astype(BF16).astype(F32)
                value = quasi[side, c, part, :] + coef_x[side, part, :] * far
                if k == 0:
                    value = value + jnp.where(line == 0, jnp.broadcast_to(added[0][c][x : x + 1], line.shape), 0.0)
                if k == ny - CHUNK:
                    value = value + jnp.where(line == CHUNK - 1, jnp.broadcast_to(added[1][c][x : x + 1], line.shape), 0.0)
                value = value.astype(BF16)
                layers[side, c, part, :] = value
                late[c, side * ny + k : side * ny + k + CHUNK, :] = value
        copies.append(pltpu.make_async_copy(layers.at[side], s2.at[:, x], sems.at[side]))
        copies[-1].start()
    for c in range(3):
        fixed = []
        for i in range(2):
            outer = rows_outer[i, c]
            base = jnp.concatenate([outer[:2], rows_middle[i, c], outer[3:4], outer[2:3]], axis=0)
            fixed.append(base + added[i][c])
        late[c, 2 * ny : 2 * ny + 2 * nx, :] = jnp.concatenate(fixed, axis=0).astype(BF16)
        for i in range(2):
            for x in range(1, nx - 1):
                fresh = jnp.broadcast_to(fixed[i][x : x + 1], line.shape)
                outer = x == 1 or x == nx - 2
                kept = blocks_outer[i, c, 0 if x == 1 else 1] if outer else blocks_middle[i, c, x - 2]
                strips[i, c, x - 1] = jnp.where(line == (CHUNK - 1) * i, fresh, kept.astype(F32)).astype(BF16)
    for i in range(2):
        place = s2.at[:, 1 : nx - 1, (ny - CHUNK) * i : (ny - CHUNK) * i + CHUNK]
        copies.append(pltpu.make_async_copy(strips.at[i], place, sems.at[2 + i]))
        copies[-1].start()
    last = gather(hot_late[...], [late[c] for c in range(3)], z_of[...])
    peak = jnp.maximum(peaks[...], last)
    slot = lax.broadcasted_iota(jnp.int32, (peak.shape[0], best.shape[0] * best.shape[1]), 1).astype(F32)
    flat = jnp.max(jnp.where(slot == slot_of[...], peak, 0.0), axis=0, keepdims=True)
    owners, each = best.shape
    place = lax.broadcasted_iota(jnp.int32, (owners, owners * each), 1)
    first = each * lax.broadcasted_iota(jnp.int32, (owners, owners * each), 0)
    wide = jnp.broadcast_to(flat, place.shape)
    for j in range(each):
        best[:, j : j + 1] = jnp.max(jnp.where(place == first + j, wide, 0.0), axis=1, keepdims=True)
    for copy in copies:
        copy.wait()


VM = pl.BlockSpec(memory_space=pltpu.VMEM)
HB = pl.BlockSpec(memory_space=pltpu.HBM)


def shape(dims, kind):
    return jax.ShapeDtypeStruct(dims, kind)


FIRST = 10**6
MIDDLE = 8 * 10**9


def call(kernel, ins, outs, scratch, mib, flops, **others):
    return pl.pallas_call(
        kernel,
        out_shape=tuple(o for o, _ in outs),
        in_specs=ins,
        out_specs=[spec for _, spec in outs],
        scratch_shapes=scratch,
        compiler_params=pltpu.CompilerParams(vmem_limit_bytes=mib * 2**20),
        cost_estimate=pl.CostEstimate(flops=flops, bytes_accessed=10**6, transcendentals=0),
        name=kernel.__name__,
        **others,
    )


def body(velocity, viscosity, tap_cell, tap_block, block_slot):
    _, nx, ny, nz = velocity.shape
    taps = tap_cell.shape[1]
    tiles = len(tiles_of(nz))
    tall = TOP + ny + 8
    groups = lax.axis_size(("gx", "gy"))
    each = block_slot.shape[0] // groups
    late_rows = 2 * ny + 2 * nx

    def perms(axis):
        peers = lax.axis_size(axis)
        up = [(i, (i + 1) % peers) for i in range(peers)]
        return up, [(j, i) for i, j in up]

    x_up, x_down = perms("gx")
    y_up, y_down = perms("gy")

    yface = (shape((4, nx, nz), BF16), VM)
    xface = (shape((4, ny, nz), BF16), VM)
    (own_lo,) = call(x_face, [HB] * 2, [xface], [pltpu.SemaphoreType.DMA((2,))], 60, 10**6)(velocity, viscosity)
    ahi = lax.ppermute(own_lo, "gx", x_down)
    own_ylo, own_yhi, own_hi = call(other_faces, [VM] * 2 + [HB], [yface, yface, xface], [], 8, 10**6)(velocity, viscosity, tap_cell)
    ylo = lax.ppermute(own_yhi, "gy", y_up)
    yhi = lax.ppermute(own_ylo, "gy", y_down)
    alo = lax.ppermute(own_hi, "gx", x_up)

    face = (shape((3, ny, nz), BF16), VM)
    outs = [
        (shape((3, nx, tiles, tall, LANES), F32), VM),
        (shape((nx, tiles, tall, LANES), F32), VM),
        (shape((3, nx - 2, ny, nz), BF16), VM),
        face,
        face,
        (shape((2, 3, nx, nz), F32), VM),
    ]
    scratch = [pltpu.VMEM((3, nx, tiles, tall, LANES), F32), pltpu.VMEM((2, 3, nx, 1, nz), F32)]
    pad, nu_pad, packed, edge_lo, edge_hi, rows = call(first_step, [VM] * 4, outs, scratch, 28, FIRST)(velocity, viscosity, ylo, yhi)
    plo = lax.ppermute(edge_hi, "gx", x_up)
    phi = lax.ppermute(edge_lo, "gx", x_down)

    whole = (shape((3, nx, ny, nz), BF16), HB)
    column = (shape((taps, 1), F32), VM)
    outs = [
        whole,
        (shape((2, 3, nx - 4, CHUNK, nz), BF16), VM),
        (shape((2, 3, nx - 4, nz), F32), VM),
        (shape((taps, 4 * ny), BF16), VM),
        (shape((taps, late_rows), BF16), VM),
        (shape((taps, 1), jnp.int32), VM),
        column,
        column,
    ]
    scratch = [
        pltpu.VMEM((3, nx - 4, ny, nz), BF16),
        pltpu.VMEM(((nx - 4) * ny, nz), BF16),
        pltpu.VMEM((2, 3, nx - 4, 1, nz), F32),
        pltpu.SemaphoreType.DMA,
    ]
    s2, blocks_middle, rows_middle, hot_outer, hot_late, z_of, slot_of, peaks = call(
        second_middle, [VM] * 4 + [HB] + [VM] * 3, outs, scratch, 28, MIDDLE
    )(pad, nu_pad, packed, viscosity, ahi, tap_cell, tap_block, block_slot[None])

    yface = (shape((3, nx, nz), BF16), VM)
    face_lo, face_hi = call(first_faces, [VM] * 6, [yface, yface], [], 4, 10**6)(rows, own_ylo, own_yhi, alo, ahi, slot_of)
    y2lo = lax.ppermute(face_hi, "gy", y_up)
    y2hi = lax.ppermute(face_lo, "gy", y_down)

    outs = [
        whole,
        (shape((2, 3, ny, nz), F32), VM),
        (shape((2, 3, ny, nz), F32), VM),
        (shape((2, 3, 4, nz), F32), VM),
        (shape((2, 3, 2, CHUNK, nz), BF16), VM),
        (shape((2, ny, nz), F32), VM),
        (shape((2, nx, nz), F32), VM),
        column,
    ]
    scratch = [
        pltpu.VMEM((3, 2, tiles, tall, LANES), F32),
        pltpu.VMEM((3, 2, ny, nz), BF16),
        pltpu.VMEM((2, tiles, tall, LANES), F32),
        pltpu.VMEM((2, 3, 1, ny, nz), BF16),
        pltpu.VMEM((4 * ny, nz), BF16),
        pltpu.VMEM((2, 3, 4, 1, nz), F32),
        pltpu.SemaphoreType.DMA((2,)),
    ]
    s2, quasi, extra, rows_outer, blocks_outer, coef_x, coef_y, peaks = call(
        second_outer, [VM] * 11 + [HB], outs, scratch, 28, 10**6, input_output_aliases={11: 0}
    )(pad, nu_pad, packed, viscosity, own_lo, own_hi, alo, ahi, hot_outer, z_of, peaks, s2)

    scratch = [
        pltpu.VMEM((2, 3, ny, nz), BF16),
        pltpu.VMEM((2, 3, nx - 2, CHUNK, nz), BF16),
        pltpu.VMEM((3, late_rows, nz), BF16),
        pltpu.SemaphoreType.DMA((4,)),
    ]
    new_velocity, best = call(
        second_edges, [VM] * 16 + [HB], [whole, (shape((groups, each), F32), VM)], scratch, 16, 10**6, input_output_aliases={16: 0}
    )(plo, phi, extra, quasi, coef_x, y2lo, y2hi, rows_middle, rows_outer, coef_y, blocks_middle, blocks_outer,
      hot_late, z_of, slot_of, peaks, s2)

    received = lax.all_to_all(best, ("gx", "gy"), split_axis=0, concat_axis=0, tiled=True)
    return new_velocity, jnp.max(received, axis=0)


def solution(mesh):
    placed = (
        P(None, "gx", "gy", None),
        P("gx", "gy", None),
        P(("gx", "gy"), None),
        P(("gx", "gy"), None),
        P(),
    )
    return jax.shard_map(
        body,
        mesh=mesh,
        in_specs=placed,
        out_specs=(P(None, "gx", "gy", None), P(("gx", "gy"))),
        check_vma=False,
    )
```

```python
import jax
import jax.numpy as jnp
from jax import lax
from jax.experimental import pallas as pl
from jax.experimental.pallas import tpu as pltpu
from jax.sharding import PartitionSpec as P

F32 = jnp.float32
BF16 = jnp.bfloat16
HALF = 0.15
TOP = 8
CHUNK = 16
LANES = 128


def tiles_of(nz):
    return [(t, min(LANES, nz - t * LANES)) for t in range(-(-nz // LANES))]


def put(pad, index, row, value):
    rows, nz = value.shape
    for t, width in tiles_of(nz):
        pad[(*index, t, slice(row, row + rows), slice(0, width))] = value[:, t * LANES : t * LANES + width]


def update(load, packed, side, ghosts, nz):
    lane = lax.broadcasted_iota(jnp.int32, (CHUNK, LANES), 1)

    def tile(t, width):
        values = [packed(f, pl.ds(t * LANES, width)) for f in range(4)]
        if width < LANES:
            values = [jnp.concatenate([v, jnp.zeros((CHUNK, LANES - width), BF16)], axis=1) for v in values]
        return values

    def wide(values):
        return [v.astype(F32) * HALF if f == 3 else v.astype(F32) for f, v in enumerate(values)]

    spans = tiles_of(nz)
    result = []
    own = tile(*spans[0])
    ahead = [pltpu.roll(v, LANES - 1, 1) for v in own]
    behind = None
    for t, width in spans:
        here = [load(f, t, 0, 0) for f in range(4)]
        current, now = ahead, own
        if t + 1 < len(spans):
            own = tile(*spans[t + 1])
            ahead = [pltpu.roll(v, LANES - 1, 1) for v in own]
            beyond = ahead
        else:
            beyond = now
        above_z = wide([jnp.where(lane == width - 1, beyond[f], current[f]) for f in range(4)])
        turned = [pltpu.roll(v, 1, 1) for v in now]
        if t:
            before = behind
        else:
            before = [jnp.zeros((CHUNK, LANES), BF16)] * 3 + [now[3]]
        below_z = wide([jnp.where(lane == 0, before[f], turned[f]) for f in range(4)])
        behind = turned
        weight = None
        terms = [[], [], []]
        for d in range(3):
            drift = here[d] * HALF
            for up in (True, False):
                missing = d == 0 and side == (1 if up else 0)
                if missing and not ghosts:
                    weight = drift if up else weight - drift
                    continue
                if d == 2:
                    far = above_z if up else below_z
                else:
                    step = 1 if up else -1
                    dx, dy = (step, 0) if d == 0 else (0, step)
                    far = [None if missing and f < 3 else load(f, t, dx, dy) for f in range(4)]
                both = far[3] + here[3]
                weight = both if weight is None else weight + both
                if far[0] is not None:
                    coef = both - drift if up else both + drift
                    for c in range(3):
                        terms[c].append(coef * far[c])
        weight = 1.0 - weight
        total = [here[c] * weight for c in range(3)]
        for c in range(3):
            for term in terms[c]:
                total[c] = total[c] + term
        result.append((here, total))
    return result


def x_face(vel, visc, lo, sems):
    copies = [pltpu.make_async_copy(vel.at[:, 0], lo.at[0:3], sems.at[0]), pltpu.make_async_copy(visc.at[0], lo.at[3], sems.at[1])]
    for copy in copies:
        copy.start()
    for copy in copies:
        copy.wait()


def other_faces(vel, visc, after, ylo, yhi, hi):
    _, nx, ny, nz = vel.shape
    hi[0:3] = vel[:, nx - 1]
    hi[3] = visc[nx - 1]
    line = lax.broadcasted_iota(jnp.int32, (nx, nz), 0)
    for i, out in enumerate((ylo, yhi)):
        rows = slice((ny - CHUNK) * i, (ny - CHUNK) * i + CHUNK)
        row = (CHUNK - 1) * i
        for f in range(4):
            total = jnp.zeros((nx, nz), F32)
            for x in range(nx):
                block = visc[x, rows] if f == 3 else vel[f, x, rows]
                one = block.astype(F32)[row : row + 1]
                total = jnp.where(line == x, jnp.broadcast_to(one, line.shape), total)
            out[f] = total.astype(BF16)


def first_step(vel, visc, ylo, yhi, next_pad, nu_pad, packed, edge_lo, edge_hi, rows, pad, lines):
    _, nx, ny, nz = vel.shape
    tiles = len(tiles_of(nz))

    def fill(x, _):
        for k in range(0, ny, CHUNK):
            for c in range(3):
                put(pad, (c, x), TOP + k, vel[c, x, k : k + CHUNK, :].astype(F32))
            put(nu_pad, (x,), TOP + k, visc[x, k : k + CHUNK, :].astype(F32) * HALF)
        return 0

    lax.fori_loop(0, nx, fill, 0)
    for ghost, row in ((ylo, TOP - 1), (yhi, TOP + ny)):
        for f in range(4):
            value = ghost[f].astype(F32) * (HALF if f == 3 else 1.0)
            for x in range(nx):
                if f == 3:
                    put(nu_pad, (x,), row, value[x : x + 1])
                else:
                    put(pad, (f, x), row, value[x : x + 1])
    for row in (0, TOP + ny):
        next_pad[:, :, :, row : row + TOP, :] = jnp.zeros((3, nx, tiles, TOP, LANES), F32)

    def layer(x, side):
        for k in range(0, ny, CHUNK):

            def load(f, t, dx, dy):
                window = pl.ds(TOP + k + dy, CHUNK)
                return nu_pad[x + dx, t, window, :] if f == 3 else pad[f, x + dx, t, window, :]

            def bits(f, part):
                return visc[x, k : k + CHUNK, part] if f == 3 else vel[f, x, k : k + CHUNK, part]

            new = update(load, bits, side, False, nz)
            for t, width in tiles_of(nz):
                part = pl.ds(t * LANES, width)
                for c in range(3):
                    value = new[t][1][c]
                    rounded = value.astype(BF16)
                    if k == 0:
                        lines[0, c, x, :, part] = value[:1, :width]
                    if k == ny - CHUNK:
                        lines[1, c, x, :, part] = value[CHUNK - 1 :, :width]
                    if side is not None:
                        (edge_lo, edge_hi)[side][c, k : k + CHUNK, part] = rounded[:, :width]
                    else:
                        value = rounded.astype(F32)
                        packed[c, x - 1, k : k + CHUNK, part] = rounded[:, :width]
                    next_pad[c, x, t, TOP + k : TOP + k + CHUNK, :] = value

    layer(0, 0)
    layer(nx - 1, 1)

    def middle(x, _):
        layer(x, None)
        return 0

    lax.fori_loop(1, nx - 1, middle, 0)
    for i in range(2):
        for c in range(3):
            for x in range(nx):
                rows[i, c, x : x + 1, :] = lines[i, c, x]


def missing_terms(mine, far, sign):
    both = (mine[3] + far[3]) * HALF
    near_coef = both - sign * HALF * mine[0]
    far_coef = both + sign * HALF * far[0]
    gaps = [far[c] - mine[c] for c in range(3)]
    return [near_coef * g for g in gaps], [-far_coef * g for g in gaps]


def first_faces(rows, own_ylo, own_yhi, alo, ahi, after, face_lo, face_hi):
    _, _, nx, nz = rows.shape
    ny = alo.shape[1]
    line = lax.broadcasted_iota(jnp.int32, (nx, nz), 0)
    for i, (own, out) in enumerate(((own_ylo, face_lo), (own_yhi, face_hi))):
        values = [rows[i, c] for c in range(3)]
        for side, ghost in enumerate((alo, ahi)):
            x = (nx - 1) * side
            k = (ny - CHUNK) * i
            row = (CHUNK - 1) * i
            mine = [own[f].astype(F32)[x : x + 1] for f in range(4)]
            far = [ghost[f, k : k + CHUNK, :].astype(F32)[row : row + 1] for f in range(4)]
            terms, _ = missing_terms(mine, far, 1.0 if side else -1.0)
            for c in range(3):
                values[c] = values[c] + jnp.where(line == x, jnp.broadcast_to(terms[c], line.shape), 0.0)
        for c in range(3):
            out[c] = values[c].astype(BF16)


def emit(new, nz, k, ny, store, strength, strength_row, blocks, lines, both_steps):
    line = lax.broadcasted_iota(jnp.int32, (CHUNK, LANES), 0)
    for t, width in tiles_of(nz):
        part = pl.ds(t * LANES, width)
        here, fresh = new[t]
        rounded = [v.astype(BF16) for v in fresh]
        energy = here[0] * here[0] + here[1] * here[1] + here[2] * here[2]
        if both_steps:
            again = [v.astype(F32) for v in rounded]
            again = again[0] * again[0] + again[1] * again[1] + again[2] * again[2]
            if k == 0:
                again = jnp.where(line == 0, 0.0, again)
            if k == ny - CHUNK:
                again = jnp.where(line == CHUNK - 1, 0.0, again)
            energy = jnp.maximum(energy, again)
        strength[pl.ds(strength_row, CHUNK), part] = energy[:, :width].astype(BF16)
        for c in range(3):
            store(c, part, fresh[c][:, :width], rounded[c][:, :width])
            if k == 0:
                lines(0, c, part, fresh[c][:1, :width])
                blocks(0, c, part, rounded[c][:, :width])
            if k == ny - CHUNK:
                lines(1, c, part, fresh[c][CHUNK - 1 :, :width])
                blocks(1, c, part, rounded[c][:, :width])


def gather(hot, energy, z):
    picked = jnp.dot(hot, energy, preferred_element_type=F32)
    lane = lax.broadcasted_iota(jnp.int32, picked.shape, 1)
    return jnp.max(jnp.where(lane == z, picked, 0.0), axis=1, keepdims=True)


def second_middle(pad, nu_pad, packed, visc, after, cells, tap_blocks, slots,
                  s2, blocks, rows, hot_outer, hot_late, z_of, slot_of, peaks, inner, strength, lines, sem):
    _, nx, tiles, _, _ = pad.shape
    ny, nz = inner.shape[2:]

    def layer(x, _):
        for k in range(0, ny, CHUNK):

            def load(f, t, dx, dy):
                window = pl.ds(TOP + k + dy, CHUNK)
                return nu_pad[x + dx, t, window, :] if f == 3 else pad[f, x + dx, t, window, :]

            def store(c, part, value, rounded):
                inner[c, x - 2, k : k + CHUNK, part] = rounded

            def put_block(i, c, part, rounded):
                blocks[i, c, x - 2, :, part] = rounded

            def put_line(i, c, part, value):
                lines[i, c, x - 2, :, part] = value

            def bits(f, part):
                return visc[x, k : k + CHUNK, part] if f == 3 else packed[f, x - 1, k : k + CHUNK, part]

            new = update(load, bits, None, True, nz)
            emit(new, nz, k, ny, store, strength, (x - 2) * ny + k, put_block, put_line, True)
        return 0

    lax.fori_loop(2, nx - 2, layer, 0)
    copy = pltpu.make_async_copy(inner, s2.at[:, 2 : nx - 2], sem)
    copy.start()
    for i in range(2):
        for c in range(3):
            for x in range(nx - 4):
                rows[i, c, x : x + 1, :] = lines[i, c, x]

    taps = cells.shape[1]
    same = lax.broadcasted_iota(jnp.int32, (taps, taps), 0) == lax.broadcasted_iota(jnp.int32, (taps, taps), 1)

    def column_of(line):
        return jnp.sum(jnp.where(same, jnp.broadcast_to(line, same.shape), 0.0), axis=1, keepdims=True)

    def one_hot(column, width):
        position = lax.broadcasted_iota(jnp.int32, (taps, width), 1)
        return jnp.where(position == column.astype(jnp.int32), 1.0, 0.0).astype(BF16)

    cell = cells[...].astype(F32)
    line_rows = jnp.floor((cell + 0.5) * (1.0 / nz))
    line_x = jnp.floor((line_rows + 0.5) * (1.0 / ny))
    line_y = line_rows - line_x * ny
    line_late = jnp.where(line_y == 0, 2 * ny + line_x, jnp.where(line_y == ny - 1, 2 * ny + nx + line_x, -1.0))
    line_late = jnp.where(line_x == 0, line_y, jnp.where(line_x == nx - 1, ny + line_y, line_late))
    row = column_of(line_rows)
    middle = row - 2 * ny
    outer = jnp.where(row < 2 * ny, row, jnp.where(row < (nx - 2) * ny, -1.0, row - (nx - 4) * ny))
    z = column_of(cell - line_rows * nz).astype(jnp.int32)
    z_of[...] = z
    hot_outer[...] = one_hot(outer, hot_outer.shape[1])
    hot_late[...] = one_hot(column_of(line_late), hot_late.shape[1])
    peaks[...] = gather(one_hot(middle, (nx - 4) * ny), strength[...], z)
    count = slots.shape[1]
    block = lax.broadcasted_iota(jnp.int32, (taps, count), 1)
    wanted = column_of(tap_blocks[...].astype(F32)).astype(jnp.int32)
    chosen = jnp.where(block == wanted, jnp.broadcast_to(slots[...].astype(F32), (taps, count)), 0.0)
    slot_of[...] = jnp.sum(chosen, axis=1, keepdims=True)
    copy.wait()


def second_outer(pad, nu_pad, packed, visc, own_lo, own_hi, alo, ahi, hot_outer, z_of, peaks_in, s2_in,
                 s2, quasi, extra, rows, blocks, coef_x, coef_y, peaks, edge, edge_bits, ghost_nu, inner, strength, lines, sems):
    _, nx, tiles, _, _ = pad.shape
    ny, nz = inner.shape[3:]
    for side, (own, ghost) in enumerate(((own_lo, alo), (own_hi, ahi))):
        x = (nx - 1) * side
        for k in range(0, ny, CHUNK):
            mine = [own[f, k : k + CHUNK, :].astype(F32) for f in range(4)]
            far = [ghost[f, k : k + CHUNK, :].astype(F32) for f in range(4)]
            terms, far_terms = missing_terms(mine, far, 1.0 if side else -1.0)
            put(ghost_nu, (side,), TOP + k, far[3] * HALF)
            for c in range(3):
                extra[side, c, k : k + CHUNK, :] = far_terms[c]
                for t, width in tiles_of(nz):
                    part = slice(t * LANES, t * LANES + width)
                    window = slice(TOP + k, TOP + k + CHUNK)
                    value = (pad[c, x, t, window, :width] + terms[c][:, part]).astype(BF16)
                    edge[c, side, t, window, :width] = value.astype(F32)
                    edge_bits[c, side, k : k + CHUNK, part] = value
    for row in (0, TOP + ny):
        edge[:, :, :, row : row + TOP, :] = jnp.zeros((3, 2, tiles, TOP, LANES), F32)

    def read(f, x, t, window):
        if f == 3:
            return ghost_nu[0, t, window, :] if x < 0 else ghost_nu[1, t, window, :] if x == nx else nu_pad[x, t, window, :]
        return edge[f, 0, t, window, :] if x == 0 else edge[f, 1, t, window, :] if x == nx - 1 else pad[f, x, t, window, :]

    for side in range(2):
        sign = 1.0 if side else -1.0
        x, beyond = (nx - 1) * side, nx if side else -1
        row, ghost_row = (TOP + ny - 1, TOP + ny) if side else (TOP, TOP - 1)
        for t, width in tiles_of(nz):
            part = pl.ds(t * LANES, width)
            for k in range(0, ny, CHUNK):
                window = slice(TOP + k, TOP + k + CHUNK)
                both = read(3, x, t, window) + read(3, beyond, t, window)
                coef_x[side, k : k + CHUNK, part] = (both - sign * HALF * read(0, x, t, window))[:, :width]
            for y in range(nx):
                window, other = slice(row, row + 1), slice(ghost_row, ghost_row + 1)
                both = read(3, y, t, window) + read(3, y, t, other)
                coef_y[side, y : y + 1, part] = (both - sign * HALF * read(1, y, t, window))[:, :width]

    for side in range(2):
        for j in range(2):
            x = (nx - 1 - j) * side + j * (1 - side)
            for k in range(0, ny, CHUNK):

                def load(f, t, dx, dy):
                    return read(f, x + dx, t, slice(TOP + k + dy, TOP + k + dy + CHUNK))

                def store(c, part, value, rounded):
                    if j:
                        inner[side, c, 0, k : k + CHUNK, part] = rounded
                    else:
                        quasi[side, c, k : k + CHUNK, part] = value

                def put_block(i, c, part, rounded):
                    if j:
                        blocks[i, c, side, :, part] = rounded

                def put_line(i, c, part, value):
                    lines[i, c, 2 * side + j, :, part] = value

                def bits(f, part):
                    if f == 3:
                        return visc[x, k : k + CHUNK, part]
                    return packed[f, x - 1, k : k + CHUNK, part] if j else edge_bits[f, side, k : k + CHUNK, part]

                new = update(load, bits, None if j else side, True, nz)
                strength_row = (2 * side + (1 - j if side else j)) * ny + k
                emit(new, nz, k, ny, store, strength, strength_row, put_block, put_line, j == 1)
    copies = [pltpu.make_async_copy(inner.at[i], s2.at[:, pl.ds(1 + (nx - 3) * i, 1)], sems.at[i]) for i in range(2)]
    for copy in copies:
        copy.start()
    for i in range(2):
        for c in range(3):
            for j in range(4):
                rows[i, c, j : j + 1, :] = lines[i, c, j]
    peaks[...] = jnp.maximum(peaks_in[...], gather(hot_outer[...], strength[...], z_of[...]))
    for copy in copies:
        copy.wait()


def second_edges(plo, phi, extra, quasi, coef_x, ylo, yhi, rows_middle, rows_outer, coef_y, blocks_middle, blocks_outer,
                 hot_late, z_of, slot_of, peaks, s2_in, s2, best, layers, strips, late, sems):
    _, _, ny, nz = quasi.shape
    nx = ylo.shape[1]
    copies = []
    added = [[coef_y[i] * g[c].astype(F32) for c in range(3)] for i, g in enumerate((ylo, yhi))]
    line = lax.broadcasted_iota(jnp.int32, (CHUNK, nz), 0)
    for side, ghost in enumerate((plo, phi)):
        x = (nx - 1) * side
        for k in range(0, ny, CHUNK):
            part = slice(k, k + CHUNK)
            energy = None
            for c in range(3):
                far = (ghost[c, part, :].astype(F32) + extra[side, c, part, :]).astype(BF16).astype(F32)
                value = quasi[side, c, part, :] + coef_x[side, part, :] * far
                if k == 0:
                    value = value + jnp.where(line == 0, jnp.broadcast_to(added[0][c][x : x + 1], line.shape), 0.0)
                if k == ny - CHUNK:
                    value = value + jnp.where(line == CHUNK - 1, jnp.broadcast_to(added[1][c][x : x + 1], line.shape), 0.0)
                value = value.astype(BF16)
                layers[side, c, part, :] = value
                value = value.astype(F32)
                energy = value * value if c == 0 else energy + value * value
            late[side * ny + k : side * ny + k + CHUNK, :] = energy.astype(BF16)
        copies.append(pltpu.make_async_copy(layers.at[side], s2.at[:, x], sems.at[side]))
        copies[-1].start()
    energy = None
    for c in range(3):
        fixed = []
        for i in range(2):
            outer = rows_outer[i, c]
            base = jnp.concatenate([outer[:2], rows_middle[i, c], outer[3:4], outer[2:3]], axis=0)
            fixed.append(base + added[i][c])
        value = jnp.concatenate(fixed, axis=0).astype(BF16).astype(F32)
        energy = value * value if c == 0 else energy + value * value
        for i in range(2):
            for x in range(1, nx - 1):
                fresh = jnp.broadcast_to(fixed[i][x : x + 1], line.shape)
                outer = x == 1 or x == nx - 2
                kept = blocks_outer[i, c, 0 if x == 1 else 1] if outer else blocks_middle[i, c, x - 2]
                strips[i, c, x - 1] = jnp.where(line == (CHUNK - 1) * i, fresh, kept.astype(F32)).astype(BF16)
    for i in range(2):
        place = s2.at[:, 1 : nx - 1, (ny - CHUNK) * i : (ny - CHUNK) * i + CHUNK]
        copies.append(pltpu.make_async_copy(strips.at[i], place, sems.at[2 + i]))
        copies[-1].start()
    late[2 * ny : 2 * ny + 2 * nx, :] = energy.astype(BF16)
    last = gather(hot_late[...], late[...], z_of[...])
    peak = jnp.maximum(peaks[...], last)
    slot = lax.broadcasted_iota(jnp.int32, (peak.shape[0], best.shape[0] * best.shape[1]), 1).astype(F32)
    flat = jnp.max(jnp.where(slot == slot_of[...], peak, 0.0), axis=0, keepdims=True)
    owners, each = best.shape
    place = lax.broadcasted_iota(jnp.int32, (owners, owners * each), 1)
    first = each * lax.broadcasted_iota(jnp.int32, (owners, owners * each), 0)
    wide = jnp.broadcast_to(flat, place.shape)
    for j in range(each):
        best[:, j : j + 1] = jnp.max(jnp.where(place == first + j, wide, 0.0), axis=1, keepdims=True)
    for copy in copies:
        copy.wait()


def final_max(received, highest):
    highest[...] = jnp.max(received[...], axis=0, keepdims=True)


VM = pl.BlockSpec(memory_space=pltpu.VMEM)
HB = pl.BlockSpec(memory_space=pltpu.HBM)


def shape(dims, kind):
    return jax.ShapeDtypeStruct(dims, kind)


FIRST = 10**6
MIDDLE = 8 * 10**9


def call(kernel, ins, outs, scratch, mib, flops, **others):
    return pl.pallas_call(
        kernel,
        out_shape=tuple(o for o, _ in outs),
        in_specs=ins,
        out_specs=[spec for _, spec in outs],
        scratch_shapes=scratch,
        compiler_params=pltpu.CompilerParams(vmem_limit_bytes=mib * 2**20),
        cost_estimate=pl.CostEstimate(flops=flops, bytes_accessed=10**6, transcendentals=0),
        name=kernel.__name__,
        **others,
    )


def body(velocity, viscosity, tap_cell, tap_block, block_slot):
    _, nx, ny, nz = velocity.shape
    taps = tap_cell.shape[1]
    tiles = len(tiles_of(nz))
    tall = TOP + ny + 8
    groups = lax.axis_size(("gx", "gy"))
    each = block_slot.shape[0] // groups
    late_rows = 2 * ny + 2 * nx

    def perms(axis):
        peers = lax.axis_size(axis)
        up = [(i, (i + 1) % peers) for i in range(peers)]
        return up, [(j, i) for i, j in up]

    x_up, x_down = perms("gx")
    y_up, y_down = perms("gy")

    yface = (shape((4, nx, nz), BF16), VM)
    xface = (shape((4, ny, nz), BF16), VM)
    (own_lo,) = call(x_face, [HB] * 2, [xface], [pltpu.SemaphoreType.DMA((2,))], 60, 10**6)(velocity, viscosity)
    ahi = lax.ppermute(own_lo, "gx", x_down)
    own_ylo, own_yhi, own_hi = call(other_faces, [VM] * 2 + [HB], [yface, yface, xface], [], 8, 10**6)(velocity, viscosity, tap_cell)
    ylo = lax.ppermute(own_yhi, "gy", y_up)
    yhi = lax.ppermute(own_ylo, "gy", y_down)
    alo = lax.ppermute(own_hi, "gx", x_up)

    face = (shape((3, ny, nz), BF16), VM)
    outs = [
        (shape((3, nx, tiles, tall, LANES), F32), VM),
        (shape((nx, tiles, tall, LANES), F32), VM),
        (shape((3, nx - 2, ny, nz), BF16), VM),
        face,
        face,
        (shape((2, 3, nx, nz), F32), VM),
    ]
    scratch = [pltpu.VMEM((3, nx, tiles, tall, LANES), F32), pltpu.VMEM((2, 3, nx, 1, nz), F32)]
    pad, nu_pad, packed, edge_lo, edge_hi, rows = call(first_step, [VM] * 4, outs, scratch, 28, FIRST)(velocity, viscosity, ylo, yhi)
    plo = lax.ppermute(edge_hi, "gx", x_up)
    phi = lax.ppermute(edge_lo, "gx", x_down)

    whole = (shape((3, nx, ny, nz), BF16), HB)
    column = (shape((taps, 1), F32), VM)
    outs = [
        whole,
        (shape((2, 3, nx - 4, CHUNK, nz), BF16), VM),
        (shape((2, 3, nx - 4, nz), F32), VM),
        (shape((taps, 4 * ny), BF16), VM),
        (shape((taps, late_rows), BF16), VM),
        (shape((taps, 1), jnp.int32), VM),
        column,
        column,
    ]
    scratch = [
        pltpu.VMEM((3, nx - 4, ny, nz), BF16),
        pltpu.VMEM(((nx - 4) * ny, nz), BF16),
        pltpu.VMEM((2, 3, nx - 4, 1, nz), F32),
        pltpu.SemaphoreType.DMA,
    ]
    s2, blocks_middle, rows_middle, hot_outer, hot_late, z_of, slot_of, peaks = call(
        second_middle, [VM] * 4 + [HB] + [VM] * 3, outs, scratch, 28, MIDDLE
    )(pad, nu_pad, packed, viscosity, ahi, tap_cell, tap_block, block_slot[None])

    yface = (shape((3, nx, nz), BF16), VM)
    face_lo, face_hi = call(first_faces, [VM] * 6, [yface, yface], [], 4, 10**6)(rows, own_ylo, own_yhi, alo, ahi, slot_of)
    y2lo = lax.ppermute(face_hi, "gy", y_up)
    y2hi = lax.ppermute(face_lo, "gy", y_down)

    outs = [
        whole,
        (shape((2, 3, ny, nz), F32), VM),
        (shape((2, 3, ny, nz), F32), VM),
        (shape((2, 3, 4, nz), F32), VM),
        (shape((2, 3, 2, CHUNK, nz), BF16), VM),
        (shape((2, ny, nz), F32), VM),
        (shape((2, nx, nz), F32), VM),
        column,
    ]
    scratch = [
        pltpu.VMEM((3, 2, tiles, tall, LANES), F32),
        pltpu.VMEM((3, 2, ny, nz), BF16),
        pltpu.VMEM((2, tiles, tall, LANES), F32),
        pltpu.VMEM((2, 3, 1, ny, nz), BF16),
        pltpu.VMEM((4 * ny, nz), BF16),
        pltpu.VMEM((2, 3, 4, 1, nz), F32),
        pltpu.SemaphoreType.DMA((2,)),
    ]
    s2, quasi, extra, rows_outer, blocks_outer, coef_x, coef_y, peaks = call(
        second_outer, [VM] * 11 + [HB], outs, scratch, 28, 10**6, input_output_aliases={11: 0}
    )(pad, nu_pad, packed, viscosity, own_lo, own_hi, alo, ahi, hot_outer, z_of, peaks, s2)

    scratch = [
        pltpu.VMEM((2, 3, ny, nz), BF16),
        pltpu.VMEM((2, 3, nx - 2, CHUNK, nz), BF16),
        pltpu.VMEM((late_rows, nz), BF16),
        pltpu.SemaphoreType.DMA((4,)),
    ]
    new_velocity, best = call(
        second_edges, [VM] * 16 + [HB], [whole, (shape((groups, each), F32), VM)], scratch, 16, 10**6, input_output_aliases={16: 0}
    )(plo, phi, extra, quasi, coef_x, y2lo, y2hi, rows_middle, rows_outer, coef_y, blocks_middle, blocks_outer,
      hot_late, z_of, slot_of, peaks, s2)

    received = lax.all_to_all(best, ("gx", "gy"), split_axis=0, concat_axis=0, tiled=True)
    (highest,) = call(final_max, [VM], [(shape((1, each), F32), VM)], [], 4, 10**6)(received)
    return new_velocity, highest[0]


def solution(mesh):
    placed = (
        P(None, "gx", "gy", None),
        P("gx", "gy", None),
        P(("gx", "gy"), None),
        P(("gx", "gy"), None),
        P(),
    )
    return jax.shard_map(
        body,
        mesh=mesh,
        in_specs=placed,
        out_specs=(P(None, "gx", "gy", None), P(("gx", "gy"))),
        check_vma=False,
    )
```
